128 devices in a mesh: attn: 16 (over y, x), ffn: 8 (over z, core).
Axes of the slice: x: 4, y: 4, z: 4, core: 2. Of those that a mesh axis runs over, the one named last changes fastest.
Arguments:
- hidden: bfloat16 [2048, 7168], P(('attn', 'ffn')), may hold values from -6 to 6
- norm_gain: float32 [7168], replicated, may hold values from 0.1 to 1.9
- expert_ids: int32 [2048, 3], P(('attn', 'ffn')), may hold values from 0 to 7, all different within a row; in each aligned block of 16 rows (0 to 15, 16 to 31, ...) at most 8 rows name the same one
- gate_scores: float32 [2048, 3], P(('attn', 'ffn')), may hold values from 0.1 to 0.6
- expert_in: bfloat16 [8, 2, 5120, 7168], P('ffn', None, 'attn'), may hold values from -0.0625 to 0.0625
- expert_out: bfloat16 [8, 5120, 7168], P('ffn', 'attn'), may hold values from -0.078125 to 0.078125
- kv_pages: bfloat16 [4096, 64, 512], P(('attn', 'ffn')), may hold values from -6 to 6
- block_table: int32 [2048, 2], P(('attn', 'ffn')), may hold values from 0 to 31, as said below
- req_len: int32 [2048], P(('attn', 'ffn')), may hold values from 1 to 128
- new_owner: int32 [2048, 1], P(('attn', 'ffn')), may hold values from 0 to 15; in each aligned block of 16 rows (0 to 15, 16 to 31, ...) at most 2 rows name the same one
Outputs:
- moved_pages: bfloat16 [4096, 2, 64, 512], P(('attn', 'ffn'))
- moved_rows: bfloat16 [4096, 7168], P(('attn', 'ffn'))
The draws below stay inside these ranges and needn't reach their ends.
Inputs may be any that keep to these rules, and one draw needn't show every extreme that they name: `expert_ids`: each row names 3 different experts; at most 8 rows of one device name the same expert, and some device has exactly 8 rows on one expert. `new_owner`: at most 2 rows of one device name the same instance, and some device has exactly 2 rows on one instance. `block_table`: the entries of the 16 rows of one device name each of that device's 16 * 2 local page slots once.
All inputs are finite; a program needn't handle non-finite values.
Results may differ from the reference program's by a relative error of at most 0.011.
Values may be sent and summed in bfloat16 or wider, within the bound.
No kernel may reach another device: no remote copies, remote signals or barrier semaphores. Data moves between devices by JAX's collectives and lax.ppermute only.
A program may use at most 128 MiB of HBM per device.

```python
import math
import jax
import jax.numpy as jnp
import numpy as np
from jax import lax

D = 7168
FFE = 5120
TOPK = 3
PAGE = 64
PAGES_REQ = 2
REQ_DEV = 16
INSTANCES = 16
EXPERTS = 8
KVW = 512
TOKR = 128
CAP = 2
NEW_SLOTS = 32
CAPX = 8
REQ_ALL = 2048
SLOTS = 4096
NEW_ALL = 4096
N_ATTN = 16
N_FFN = 8


def draw_block_table(key, part):
    key = jax.random.fold_in(key, 7)
    device_count = REQ_ALL // REQ_DEV
    device_keys = jax.random.split(key, device_count)

    def shuffled(device_key):
        return jax.random.permutation(device_key, REQ_DEV * PAGES_REQ)
    tables = jax.vmap(shuffled)(device_keys)
    return tables.reshape(REQ_ALL, PAGES_REQ).astype(jnp.int32)


def touch_ends(result, rng, low, high):
    spot = [jax.random.randint(jax.random.fold_in(rng, axis), (), 0, length) for axis, length in enumerate(result.shape)]
    longest = result.shape.index(max(result.shape))
    neighbour = spot[:longest] + [(spot[longest] + 1) % result.shape[longest]] + spot[longest + 1:]
    return result.at[tuple(spot)].set(low).at[tuple(neighbour)].set(high)


def shard_levels(stream_key, extent, cuts, smallest, top_value):
    loudness = 1.0
    for dim, blocks in cuts:
        draws = jax.random.uniform(jax.random.fold_in(jax.random.fold_in(stream_key, 6), dim), (blocks,), jnp.float32, smallest / len(cuts), top_value / len(cuts))
        loudness = loudness * jnp.repeat(jnp.exp(draws), extent[dim] // blocks).reshape((-1,) + (1,) * (len(extent) - 1 - dim))
    return loudness


def assign_block(stream_key, own, number, rows, number_of, top, reach, skew):
    ranking = jax.random.permutation(stream_key, number_of)
    crowded, common = load_shares(number_of, rows * top, reach, skew, True), load_shares(number_of, rows * top, reach, skew, False)
    places = jnp.arange(number_of)

    def named(lengths, rotation):
        used = int((lengths > 0).sum())
        fixed = max(1, used // 4)
        passed = fixed + (places - fixed + rotation * (used - fixed)) % max(1, number_of - fixed)
        return jnp.zeros((number_of,), jnp.int32).at[ranking[jnp.where(places < fixed, places, passed)]].set(jnp.asarray(lengths, jnp.int32))

    lengths = jnp.where(number % 4 == 0, named(crowded, number // 4), named(common, number - number // 4 - 1))
    mixed = jax.random.permutation(jax.random.fold_in(own, 3), number_of)
    source_of, sink = mixed[0:number_of // 2 * 2:2], mixed[1:number_of // 2 * 2:2]
    margin = jnp.minimum(lengths[source_of] - 1, reach - lengths[sink]) // 2
    margin = jnp.where((source_of == ranking[0]) | (sink == ranking[0]) | (lengths[sink] == 0), 0, jnp.maximum(margin, 0))
    passed = jax.random.randint(jax.random.fold_in(own, 4), (number_of // 2,), 0, 1 << 20) % (margin + 1)
    lengths = lengths.at[source_of].add(-passed).at[sink].add(passed)
    labels = jnp.searchsorted(jnp.cumsum(lengths), jnp.arange(rows * top), side="right").astype(jnp.int32)
    listing = labels.reshape(top, rows).T
    listing = listing[jax.random.permutation(jax.random.fold_in(own, 1), rows)]
    rotation = jax.random.randint(jax.random.fold_in(own, 2), (rows, 1), 0, top)
    return jnp.take_along_axis(listing, (jnp.arange(top)[None, :] + rotation) % top, axis=1)


def load_shares(amount, total, limit, slope, full):
    loads = [(1 << 20) // math.isqrt(grade ** slope) + 1 for grade in range(1, amount + 1)]
    largest = limit if full else min(limit, max(-(-total // amount), total * loads[0] // sum(loads)))
    least = 1 if total - largest >= amount - 1 else 0
    counts, spare = [largest] + [least] * (amount - 1), total - largest - least * (amount - 1)
    while spare > 0:
        free = [i for i in range(1, amount) if counts[i] < largest] or [i for i in range(1, amount) if counts[i] < limit]
        mass, remaining = sum([loads[i] for i in free]), spare
        for i in free:
            more = min(limit - counts[i], max(1, remaining * loads[i] // mass), spare)
            counts[i] = counts[i] + more
            spare = spare - more
    return np.array(counts)


def gaussian(own_key, dims, spread, most, cuts=(), kind=jnp.bfloat16):
    array = spread * jax.random.normal(own_key, dims, jnp.float32)
    if cuts:
        array = array * shard_levels(own_key, dims, cuts, -0.22, 0.18)
    return jnp.clip(array, -most, most).astype(kind)


def setup_inputs(seed: int = 0) -> dict:
    streams_of = jax.random.split(jax.random.key(seed), 11)
    hidden = gaussian(streams_of[0], (REQ_ALL, D), 1.0, 6.0, ((0, 128),))
    norm_gain = jnp.clip(1.0 + 0.18 * jax.random.normal(streams_of[1], (D,), jnp.float32), 0.1, 1.9)
    expert_ids_keys = jax.random.split(jax.random.fold_in(streams_of[2], 1), REQ_ALL // REQ_DEV)
    expert_ids_turns = jax.random.permutation(jax.random.fold_in(streams_of[2], 3), REQ_ALL // REQ_DEV)
    expert_ids = jax.vmap(lambda own, number: assign_block(jax.random.fold_in(streams_of[2], 2), own, number, REQ_DEV, EXPERTS, TOPK, CAPX, 2))(expert_ids_keys, expert_ids_turns).reshape((REQ_ALL, TOPK))
    gate_scores = jnp.clip(0.1 + 0.5 * jax.random.uniform(streams_of[3], (REQ_ALL, TOPK), jnp.float32) ** shard_levels(streams_of[3], (REQ_ALL, TOPK), ((0, 128),), -0.2, 0.2), 0.1, 0.6)
    expert_in = gaussian(streams_of[4], (EXPERTS, 2, FFE, D), D ** -0.5, 0.0625, ((0, 8), (2, 16)))
    expert_out = gaussian(streams_of[5], (EXPERTS, FFE, D), FFE ** -0.5, 0.078125, ((0, 8), (1, 16)))
    kv_pages = gaussian(streams_of[6], (SLOTS, PAGE, KVW), 1.0, 6.0, ((0, 128),))
    block_table = draw_block_table(jax.random.fold_in(streams_of[10], 71), 0)
    req_len = touch_ends(jax.random.randint(streams_of[8], (REQ_ALL,), 1, TOKR + 1), jax.random.fold_in(streams_of[8], 1), 1, TOKR).astype(jnp.int32)
    new_owner_keys = jax.random.split(jax.random.fold_in(streams_of[9], 1), REQ_ALL // REQ_DEV)
    new_owner_turns = jax.random.permutation(jax.random.fold_in(streams_of[9], 3), REQ_ALL // REQ_DEV)
    new_owner = jax.vmap(lambda own, number: assign_block(jax.random.fold_in(streams_of[9], 2), own, number, REQ_DEV, INSTANCES, 1, CAP, 2))(new_owner_keys, new_owner_turns).reshape((REQ_ALL, 1))
    return {"hidden": hidden, "norm_gain": norm_gain, "expert_ids": expert_ids, "gate_scores": gate_scores, "expert_in": expert_in, "expert_out": expert_out, "kv_pages": kv_pages, "block_table": block_table, "req_len": req_len, "new_owner": new_owner}


def one_expert(operands):
    expert_input, weight_in, weight_out = operands
    hidden_units = weight_out.shape[0]
    gate_up = jnp.dot(expert_input, weight_in.reshape(2 * hidden_units, -1).T, preferred_element_type=jnp.float32)
    activated = (jax.nn.silu(gate_up[:, :hidden_units]) * gate_up[:, hidden_units:]).astype(jnp.bfloat16)
    width_block = hidden_units // N_ATTN

    def add_block(step, running):
        offset = jnp.asarray(step, jnp.int32) * width_block
        act_block = lax.dynamic_slice_in_dim(activated, offset, width_block, 1)
        out_block = lax.dynamic_slice_in_dim(weight_out, offset, width_block, 0)
        product = jnp.dot(act_block, out_block, preferred_element_type=jnp.float32).astype(jnp.bfloat16)
        return running + product.astype(jnp.float32)
    start_sum = jnp.zeros((expert_input.shape[0], weight_out.shape[1]), jnp.float32)
    total = lax.fori_loop(0, N_ATTN, add_block, start_sum)
    return total.astype(jnp.bfloat16)

def reference(hidden, norm_gain, expert_ids, gate_scores, expert_in, expert_out, kv_pages, block_table, req_len, new_owner):
    shards = N_ATTN * N_FFN
    rows_all = hidden.shape[0]
    req_dev = rows_all // shards
    topk = expert_ids.shape[1]
    experts = expert_in.shape[0]
    width = hidden.shape[1]
    floats = hidden.astype(jnp.float32)
    scale = lax.rsqrt(lax.optimization_barrier(jnp.mean(floats * floats, axis=-1, keepdims=True)) + 1e-06)
    normed = (floats * scale * norm_gain).astype(jnp.bfloat16)
    pair_ids = expert_ids.reshape(shards, req_dev * topk)
    onehot = (pair_ids[:, :, None] == jnp.arange(experts, dtype=jnp.int32)[None, None, :]).astype(jnp.int32)
    rank_pos = lax.optimization_barrier(jnp.sum((jnp.cumsum(onehot, axis=1) - onehot) * onehot, axis=-1))
    device_ids = jnp.arange(shards, dtype=jnp.int32)[:, None]
    flat_slot = (pair_ids * (shards * CAPX) + device_ids * CAPX + rank_pos).reshape(-1).astype(jnp.int32)
    repeated = jnp.repeat(normed, topk, axis=0)
    buffers = jnp.zeros((experts * shards * CAPX, width), jnp.bfloat16).at[flat_slot].set(repeated)
    outputs = lax.map(one_expert, (buffers.reshape(experts, shards * CAPX, width), expert_in, expert_out))
    picked = outputs.reshape(experts * shards * CAPX, width)[flat_slot].astype(jnp.float32)
    picked = picked.reshape(rows_all, topk, width)
    updated = (floats + lax.optimization_barrier(jnp.sum(gate_scores[:, :, None] * picked, axis=1))).astype(jnp.bfloat16)
    owners = new_owner.reshape(shards, req_dev)
    owner_hot = (owners[:, :, None] == jnp.arange(N_ATTN, dtype=jnp.int32)[None, None, :]).astype(jnp.int32)
    owner_rank = lax.optimization_barrier(jnp.sum((jnp.cumsum(owner_hot, axis=1) - owner_hot) * owner_hot, axis=-1))
    inst_ids = device_ids // N_FFN
    member_ids = device_ids % N_FFN
    destination = ((owners * N_FFN + member_ids) * NEW_SLOTS + inst_ids * CAP + owner_rank).reshape(-1).astype(jnp.int32)
    slots_dev = req_dev * PAGES_REQ
    page_index = (device_ids[:, :, None] * slots_dev + block_table.reshape(shards, req_dev, PAGES_REQ)).reshape(rows_all, PAGES_REQ)
    page_rows = kv_pages[page_index.astype(jnp.int32)]
    positions = jnp.arange(PAGES_REQ, dtype=jnp.int32)[:, None] * PAGE + jnp.arange(PAGE, dtype=jnp.int32)[None, :]
    kept_mask = positions[None, :, :] < req_len[:, None, None]
    page_rows = jnp.where(kept_mask[..., None], page_rows, jnp.zeros_like(page_rows))
    moved_pages = jnp.zeros((NEW_ALL,) + page_rows.shape[1:], jnp.bfloat16).at[destination].set(page_rows)
    moved_rows = jnp.zeros((NEW_ALL, width), jnp.bfloat16).at[destination].set(updated)
    return (moved_pages, moved_rows)
```

```python
import functools

import jax
import jax.numpy as jnp
from jax import lax
from jax.experimental import pallas as pl
from jax.experimental.pallas import tpu as pltpu
from jax.sharding import PartitionSpec as P

PAGE = 64
PAGES_REQ = 2
ID_LANES = 128
MIB = 1 << 20


def expert_kernel(width, hidden_dev, req_dev, cap, member_ref, rows_ref, win_ref, wout_ref, out_ref, acc_ref):
    rows = rows_ref.shape[0]
    slots = out_ref.shape[0]
    chunk = 1024
    acc_ref[...] = jnp.zeros_like(acc_ref)

    def up(step, carry):
        cols = pl.ds(pl.multiple_of(step * chunk, chunk), chunk)
        acc_ref[...] += lax.dot_general(
            rows_ref[:, cols],
            win_ref[:, cols],
            (((1,), (1,)), ((), ())),
            preferred_element_type=jnp.float32,
        )
        return carry

    lax.fori_loop(0, width // chunk, up, 0)
    gate = acc_ref[:, :hidden_dev]
    act = (gate / (1.0 + jnp.exp(-gate)) * acc_ref[:, hidden_dev : 2 * hidden_dev]).astype(jnp.bfloat16)
    ids = rows_ref[:, width : width + ID_LANES].astype(jnp.float32)
    member = member_ref[0].astype(jnp.float32)
    hit = jnp.max(jnp.where(ids == member, 1.0, 0.0), axis=1, keepdims=True)
    first = lax.broadcasted_iota(jnp.int32, (rows, rows), 0)
    second = lax.broadcasted_iota(jnp.int32, (rows, rows), 1)
    before = jnp.where((second < first) & (second // req_dev == first // req_dev), 1.0, 0.0)
    rank = jnp.dot(
        before.astype(jnp.bfloat16),
        jnp.broadcast_to(hit, (rows, 128)).astype(jnp.bfloat16),
        preferred_element_type=jnp.float32,
    )[:, :1]
    block = lax.broadcasted_iota(jnp.int32, (rows, 1), 0) // req_dev
    place = jnp.where(hit > 0.0, block * cap + rank.astype(jnp.int32), -1)
    chosen = jnp.where(place == lax.broadcasted_iota(jnp.int32, (rows, slots), 1), 1.0, 0.0)
    picked = jnp.dot(
        jnp.transpose(chosen).astype(jnp.bfloat16), act, preferred_element_type=jnp.float32
    ).astype(jnp.bfloat16)

    def down(step, carry):
        cols = pl.ds(pl.multiple_of(step * chunk, chunk), chunk)
        out_ref[:, cols] = jnp.dot(
            picked, wout_ref[:, cols], preferred_element_type=jnp.float32
        ).astype(out_ref.dtype)
        return carry

    lax.fori_loop(0, width // chunk, down, 0)


def run_experts(member, rows, weight_in, weight_out, req_dev, cap, devices):
    width = weight_in.shape[1]
    hidden_dev = weight_out.shape[0]
    steps = 4
    block = rows.shape[0] // steps
    slots = devices * cap // steps
    once = pl.Buffered(1)
    return pl.pallas_call(
        functools.partial(expert_kernel, width, hidden_dev, req_dev, cap),
        out_shape=jax.ShapeDtypeStruct((devices * cap, width), jnp.bfloat16),
        grid=(steps,),
        in_specs=[
            pl.BlockSpec(memory_space=pltpu.SMEM),
            pl.BlockSpec((block, rows.shape[1]), lambda s: (s, 0)),
            pl.BlockSpec(weight_in.shape, lambda s: (0, 0), pipeline_mode=once),
            pl.BlockSpec(weight_out.shape, lambda s: (0, 0), pipeline_mode=once),
        ],
        out_specs=pl.BlockSpec((slots, width), lambda s: (s, 0)),
        scratch_shapes=[pltpu.VMEM((block, 2 * hidden_dev), jnp.float32)],
        compiler_params=pltpu.CompilerParams(vmem_limit_bytes=56 * MIB),
        cost_estimate=pl.CostEstimate(
            flops=2 * rows.shape[0] * width * 2 * hidden_dev + 2 * devices * cap * width * hidden_dev,
            bytes_accessed=2 * (rows.size + weight_in.size + weight_out.size + devices * cap * width),
            transcendentals=rows.shape[0] * hidden_dev,
        ),
    )(member, rows, weight_in, weight_out)


def body(
    hidden,
    norm_gain,
    expert_ids,
    gate_scores,
    expert_in,
    expert_out,
    kv_pages,
    block_table,
    req_len,
    new_owner,
):
    req_dev = hidden.shape[0]
    width = hidden.shape[1]
    topk = expert_ids.shape[1]
    members = lax.axis_size("ffn")
    instances = lax.axis_size("attn")
    expert_cap = req_dev * topk * 4 // (members * 3)
    per_peer = 2 * req_dev // instances

    floats = hidden.astype(jnp.float32)
    scale = lax.rsqrt(jnp.mean(floats * floats, axis=-1, keepdims=True) + 1e-06)
    normed = (floats * scale * norm_gain).astype(jnp.bfloat16)
    id_lanes = jnp.pad(expert_ids, ((0, 0), (0, ID_LANES - topk)), constant_values=-1)
    payload = jnp.concatenate([normed, id_lanes.astype(jnp.bfloat16)], axis=1)
    payload, kv_pages = lax.optimization_barrier((payload, kv_pages))
    gathered = lax.all_gather(payload, ("attn", "ffn"), axis=0, tiled=True)

    owners = new_owner.reshape(-1)
    owner_hot = (owners[:, None] == jnp.arange(instances, dtype=jnp.int32)[None, :]).astype(
        jnp.int32
    )
    owner_rank = jnp.sum((jnp.cumsum(owner_hot, axis=0) - owner_hot) * owner_hot, axis=1)
    send_slot = owners * per_peer + owner_rank
    routing = jnp.arange(instances * per_peer, dtype=jnp.int32)[:, None] == send_slot[None, :]
    occupied = jnp.any(routing, axis=1)
    sources = jnp.sum(
        routing.astype(jnp.int32) * jnp.arange(req_dev, dtype=jnp.int32)[None, :], axis=1
    )
    tables = block_table[sources]
    page_rows = kv_pages[tables]
    positions = (
        jnp.arange(PAGES_REQ, dtype=jnp.int32)[:, None] * PAGE
        + jnp.arange(PAGE, dtype=jnp.int32)[None, :]
    )
    kept_mask = (positions[None, :, :] < req_len[sources][:, None, None]) & occupied[:, None, None]
    outgoing_pages = jnp.where(kept_mask[..., None], page_rows, jnp.zeros_like(page_rows))
    moved_pages = lax.all_to_all(outgoing_pages, "attn", split_axis=0, concat_axis=0, tiled=True)

    gathered, moved_pages = lax.optimization_barrier((gathered, moved_pages))
    member = lax.axis_index("ffn").astype(jnp.int32).reshape(1)
    hidden_dev = expert_in.shape[2]
    partial = run_experts(
        member,
        gathered,
        expert_in.reshape(2 * hidden_dev, width),
        expert_out.reshape(hidden_dev, width),
        req_dev,
        expert_cap,
        members * instances,
    )
    summed = lax.psum_scatter(partial, "attn", scatter_dimension=0, tiled=True)
    results = summed.reshape(members, expert_cap, width)
    returned = lax.all_to_all(results, "ffn", split_axis=0, concat_axis=0, tiled=True)

    pair_ids = expert_ids.reshape(-1)
    onehot = (pair_ids[:, None] == jnp.arange(members, dtype=jnp.int32)[None, :]).astype(jnp.int32)
    rank_pos = jnp.sum((jnp.cumsum(onehot, axis=0) - onehot) * onehot, axis=1)
    slot_ids = pair_ids * expert_cap + rank_pos
    matches = jnp.arange(members * expert_cap, dtype=jnp.int32)[:, None] == slot_ids[None, :]
    matches = matches.reshape(members * expert_cap, req_dev, topk)
    combine_weights = jnp.einsum(
        "sjk,jk->js", matches.astype(jnp.float32), gate_scores, precision=lax.Precision.HIGHEST
    )
    expert_mix = jnp.dot(
        combine_weights,
        returned.reshape(members * expert_cap, width).astype(jnp.float32),
        precision=lax.Precision.HIGHEST,
    )
    updated = (floats + expert_mix).astype(jnp.bfloat16)
    rows_out = jnp.dot(
        routing.astype(jnp.bfloat16), updated, preferred_element_type=jnp.float32
    ).astype(jnp.bfloat16)
    moved_rows = lax.all_to_all(rows_out, "attn", split_axis=0, concat_axis=0, tiled=True)
    return (moved_pages, moved_rows)


def solution(mesh):
    in_specs = (
        P(("attn", "ffn"), None),
        P(),
        P(("attn", "ffn"), None),
        P(("attn", "ffn"), None),
        P("ffn", None, "attn", None),
        P("ffn", "attn", None),
        P(("attn", "ffn"), None, None),
        P(("attn", "ffn"), None),
        P(("attn", "ffn")),
        P(("attn", "ffn"), None),
    )
    out_specs = (P(("attn", "ffn"), None, None, None), P(("attn", "ffn"), None))
    return jax.shard_map(body, mesh=mesh, in_specs=in_specs, out_specs=out_specs, check_vma=False)
```

```python
import functools

import jax
import jax.numpy as jnp
from jax import lax
from jax.experimental import pallas as pl
from jax.experimental.pallas import tpu as pltpu
from jax.sharding import PartitionSpec as P

PAGE = 64
PAGES_REQ = 2
ID_LANES = 128
MIB = 1 << 20


def expert_kernel(
    width, hidden_dev, req_dev, cap, chunk, parts, member_ref, rows_ref, win_hbm, wout_hbm, out_ref, acc_ref, pick_ref, win_ref, wout_ref, sems
):
    rows = rows_ref.shape[0]
    slots = out_ref.shape[0]
    count = width // chunk
    at_start = pl.program_id(0) == 0

    def win_copy(step):
        cols = pl.ds(pl.multiple_of(step * chunk, chunk), chunk)
        return pltpu.make_async_copy(win_hbm.at[:, cols], win_ref.at[:, cols], sems.at[step])

    def wout_copy():
        return pltpu.make_async_copy(wout_hbm, wout_ref, sems.at[count])

    @pl.when(at_start)
    def _():
        for step in range(count):
            win_copy(step).start()
        wout_copy().start()

    ids = rows_ref[:, width : width + ID_LANES].astype(jnp.float32)
    member = member_ref[0].astype(jnp.float32)
    hit = jnp.max(jnp.where(ids == member, 1.0, 0.0), axis=1, keepdims=True)
    first = lax.broadcasted_iota(jnp.int32, (rows, rows), 0)
    second = lax.broadcasted_iota(jnp.int32, (rows, rows), 1)
    before = jnp.where((second < first) & (second // req_dev == first // req_dev), 1.0, 0.0)
    rank = jnp.dot(
        before.astype(jnp.bfloat16),
        jnp.broadcast_to(hit, (rows, 128)).astype(jnp.bfloat16),
        preferred_element_type=jnp.float32,
    )[:, :1]
    block = lax.broadcasted_iota(jnp.int32, (rows, 1), 0) // req_dev
    place = jnp.where(hit > 0.0, block * cap + rank.astype(jnp.int32), -1)
    chosen = jnp.where(place == lax.broadcasted_iota(jnp.int32, (rows, slots), 1), 1.0, 0.0)
    pick_ref[...] = jnp.transpose(chosen).astype(jnp.bfloat16)
    acc_ref[...] = jnp.zeros_like(acc_ref)
    part_rows, part_slots = rows // parts, slots // parts

    def up(step, carry):
        cols = pl.ds(pl.multiple_of(step * chunk, chunk), chunk)

        @pl.when(at_start)
        def _():
            win_copy(step).wait()

        picked = [
            jnp.dot(
                pick_ref[i * part_slots : (i + 1) * part_slots, i * part_rows : (i + 1) * part_rows],
                rows_ref[i * part_rows : (i + 1) * part_rows, cols],
                preferred_element_type=jnp.float32,
            ).astype(jnp.bfloat16)
            for i in range(parts)
        ]
        acc_ref[...] += lax.dot_general(
            jnp.concatenate(picked, axis=0),
            win_ref[:, cols],
            (((1,), (1,)), ((), ())),
            preferred_element_type=jnp.float32,
        )
        return carry

    lax.fori_loop(0, count, up, 0, unroll=count)
    gate = acc_ref[:, :hidden_dev]
    act = (gate / (1.0 + jnp.exp(-gate)) * acc_ref[:, hidden_dev : 2 * hidden_dev]).astype(jnp.bfloat16)

    @pl.when(at_start)
    def _():
        wout_copy().wait()

    def down(step, carry):
        cols = pl.ds(pl.multiple_of(step * chunk, chunk), chunk)
        out_ref[:, cols] = jnp.dot(
            act, wout_ref[:, cols], preferred_element_type=jnp.float32
        ).astype(out_ref.dtype)
        return carry

    lax.fori_loop(0, count, down, 0, unroll=count)


def run_experts(member, rows, weight_in, weight_out, req_dev, cap, devices):
    width = weight_in.shape[1]
    hidden_dev = weight_out.shape[0]
    steps, parts, chunk = 4, 2, width // 4
    block = rows.shape[0] // steps
    slots = devices * cap // steps
    return pl.pallas_call(
        functools.partial(expert_kernel, width, hidden_dev, req_dev, cap, chunk, parts),
        out_shape=jax.ShapeDtypeStruct((devices * cap, width), jnp.bfloat16),
        grid=(steps,),
        in_specs=[
            pl.BlockSpec(memory_space=pltpu.SMEM),
            pl.BlockSpec((block, rows.shape[1]), lambda s: (s, 0)),
            pl.BlockSpec(memory_space=pl.ANY),
            pl.BlockSpec(memory_space=pl.ANY),
        ],
        out_specs=pl.BlockSpec((slots, width), lambda s: (s, 0)),
        scratch_shapes=[
            pltpu.VMEM((slots, 2 * hidden_dev), jnp.float32),
            pltpu.VMEM((slots, block), jnp.bfloat16),
            pltpu.VMEM(weight_in.shape, weight_in.dtype),
            pltpu.VMEM(weight_out.shape, weight_out.dtype),
            pltpu.SemaphoreType.DMA((width // chunk + 1,)),
        ],
        compiler_params=pltpu.CompilerParams(vmem_limit_bytes=56 * MIB),
        cost_estimate=pl.CostEstimate(
            flops=2 * devices * cap * width * (3 * hidden_dev + 2 * req_dev * 8),
            bytes_accessed=2 * (rows.size + weight_in.size + weight_out.size + devices * cap * width),
            transcendentals=devices * cap * hidden_dev,
        ),
    )(member, rows, weight_in, weight_out)


def body(
    hidden,
    norm_gain,
    expert_ids,
    gate_scores,
    expert_in,
    expert_out,
    kv_pages,
    block_table,
    req_len,
    new_owner,
):
    req_dev = hidden.shape[0]
    width = hidden.shape[1]
    topk = expert_ids.shape[1]
    members = lax.axis_size("ffn")
    instances = lax.axis_size("attn")
    expert_cap = req_dev * topk * 4 // (members * 3)
    per_peer = 2 * req_dev // instances

    floats = hidden.astype(jnp.float32)
    scale = lax.rsqrt(jnp.mean(floats * floats, axis=-1, keepdims=True) + 1e-06)
    normed = (floats * scale * norm_gain).astype(jnp.bfloat16)
    id_lanes = jnp.pad(expert_ids, ((0, 0), (0, ID_LANES - topk)), constant_values=-1)
    payload = jnp.concatenate([normed, id_lanes.astype(jnp.bfloat16)], axis=1)
    payload, kv_pages = lax.optimization_barrier((payload, kv_pages))
    gathered = lax.all_gather(payload, ("attn", "ffn"), axis=0, tiled=True)

    owners = new_owner.reshape(-1)
    owner_hot = (owners[:, None] == jnp.arange(instances, dtype=jnp.int32)[None, :]).astype(
        jnp.int32
    )
    owner_rank = jnp.sum((jnp.cumsum(owner_hot, axis=0) - owner_hot) * owner_hot, axis=1)
    send_slot = owners * per_peer + owner_rank
    routing = jnp.arange(instances * per_peer, dtype=jnp.int32)[:, None] == send_slot[None, :]
    occupied = jnp.any(routing, axis=1)
    sources = jnp.sum(
        routing.astype(jnp.int32) * jnp.arange(req_dev, dtype=jnp.int32)[None, :], axis=1
    )
    tables = block_table[sources]
    page_rows = kv_pages[tables]
    positions = (
        jnp.arange(PAGES_REQ, dtype=jnp.int32)[:, None] * PAGE
        + jnp.arange(PAGE, dtype=jnp.int32)[None, :]
    )
    kept_mask = (positions[None, :, :] < req_len[sources][:, None, None]) & occupied[:, None, None]
    outgoing_pages = jnp.where(kept_mask[..., None], page_rows, jnp.zeros_like(page_rows))
    first_pages = lax.all_to_all(outgoing_pages[:, 0], "attn", split_axis=0, concat_axis=0, tiled=True)
    gathered, first_pages, second_out = lax.optimization_barrier(
        (gathered, first_pages, outgoing_pages[:, 1])
    )
    second_pages = lax.all_to_all(second_out, "attn", split_axis=0, concat_axis=0, tiled=True)
    member = lax.axis_index("ffn").astype(jnp.int32).reshape(1)
    hidden_dev = expert_in.shape[2]
    partial = run_experts(
        member,
        gathered,
        expert_in.reshape(2 * hidden_dev, width),
        expert_out.reshape(hidden_dev, width),
        req_dev,
        expert_cap,
        members * instances,
    )
    moved_pages = jnp.stack([first_pages, second_pages], axis=1)
    partial, moved_pages = lax.optimization_barrier((partial, moved_pages))
    summed = lax.psum_scatter(partial, "attn", scatter_dimension=0, tiled=True)
    results = summed.reshape(members, expert_cap, width)
    returned = lax.all_to_all(results, "ffn", split_axis=0, concat_axis=0, tiled=True)

    pair_ids = expert_ids.reshape(-1)
    onehot = (pair_ids[:, None] == jnp.arange(members, dtype=jnp.int32)[None, :]).astype(jnp.int32)
    rank_pos = jnp.sum((jnp.cumsum(onehot, axis=0) - onehot) * onehot, axis=1)
    slot_ids = pair_ids * expert_cap + rank_pos
    matches = jnp.arange(members * expert_cap, dtype=jnp.int32)[:, None] == slot_ids[None, :]
    matches = matches.reshape(members * expert_cap, req_dev, topk)
    combine_weights = jnp.einsum(
        "sjk,jk->js", matches.astype(jnp.float32), gate_scores, precision=lax.Precision.HIGHEST
    )
    expert_mix = jnp.dot(
        combine_weights,
        returned.reshape(members * expert_cap, width).astype(jnp.float32),
        precision=lax.Precision.HIGHEST,
    )
    updated = (floats + expert_mix).astype(jnp.bfloat16)
    rows_out = jnp.dot(
        routing.astype(jnp.bfloat16), updated, preferred_element_type=jnp.float32
    ).astype(jnp.bfloat16)
    moved_rows = lax.all_to_all(rows_out, "attn", split_axis=0, concat_axis=0, tiled=True)
    return (moved_pages, moved_rows)


def solution(mesh):
    in_specs = (
        P(("attn", "ffn"), None),
        P(),
        P(("attn", "ffn"), None),
        P(("attn", "ffn"), None),
        P("ffn", None, "attn", None),
        P("ffn", "attn", None),
        P(("attn", "ffn"), None, None),
        P(("attn", "ffn"), None),
        P(("attn", "ffn")),
        P(("attn", "ffn"), None),
    )
    out_specs = (P(("attn", "ffn"), None, None, None), P(("attn", "ffn"), None))
    return jax.shard_map(body, mesh=mesh, in_specs=in_specs, out_specs=out_specs, check_vma=False)
```

```python
import functools

import jax
import jax.numpy as jnp
from jax import lax
from jax.experimental import pallas as pl
from jax.experimental.pallas import tpu as pltpu
from jax.sharding import PartitionSpec as P

PAGE = 64
PAGES_REQ = 2
ID_LANES = 128
MIB = 1 << 20


def expert_kernel(
    hidden_dev, req_dev, cap, topk, up_steps,
    member_ref, lanes_ref, rows_ref, win_ref, wout_ref,
    main_ref, gated_ref,
    acc_ref, chosen_ref, pick_ref, picked_ref, act_ref,
):
    step = pl.program_id(0)
    groups, slots, rows = pick_ref.shape
    member = member_ref[0].astype(jnp.float32)

    @pl.when(step == 0)
    def _():
        first = lax.broadcasted_iota(jnp.int32, (rows, rows), 0)
        second = lax.broadcasted_iota(jnp.int32, (rows, rows), 1)
        before = jnp.where((second < first) & (second // req_dev == first // req_dev), 1.0, 0.0)
        block = lax.broadcasted_iota(jnp.int32, (rows, 1), 0) // req_dev
        slot = lax.broadcasted_iota(jnp.int32, (rows, slots), 1)
        for group in range(groups):
            lanes = lanes_ref[group * rows : (group + 1) * rows, :].astype(jnp.float32)
            lane = lax.broadcasted_iota(jnp.int32, lanes.shape, 1)
            hit = jnp.max(jnp.where((lanes == member) & (lane < topk), 1.0, 0.0), axis=1, keepdims=True)
            rank = jnp.dot(
                before.astype(jnp.bfloat16),
                jnp.broadcast_to(hit, (rows, 128)).astype(jnp.bfloat16),
                preferred_element_type=jnp.float32,
            )[:, :1]
            place = jnp.where(hit > 0.0, block * cap + rank.astype(jnp.int32), -1)
            chosen = jnp.where(place == slot, 1.0, 0.0)
            chosen_ref[group] = chosen.astype(jnp.bfloat16)
            pick_ref[group] = jnp.transpose(chosen).astype(jnp.bfloat16)
        acc_ref[...] = jnp.zeros_like(acc_ref)

    @pl.when(step < up_steps)
    def _():
        for group in range(groups):
            picked_ref[group * slots : (group + 1) * slots, :] = jnp.dot(
                pick_ref[group],
                rows_ref[group * rows : (group + 1) * rows, :],
                preferred_element_type=jnp.float32,
            ).astype(jnp.bfloat16)
        acc_ref[...] += lax.dot_general(
            picked_ref[...], win_ref[...], (((1,), (1,)), ((), ())), preferred_element_type=jnp.float32
        )

    @pl.when(step == up_steps - 1)
    def _():
        gate = acc_ref[:, :hidden_dev]
        act_ref[...] = (gate / (1.0 + jnp.exp(-gate)) * acc_ref[:, hidden_dev : 2 * hidden_dev]).astype(jnp.bfloat16)
        for group in range(groups):
            lanes = lanes_ref[group * rows : (group + 1) * rows, :].astype(jnp.float32)
            score = jnp.zeros((rows, 1), jnp.float32)
            for k in range(topk):
                high, low = (lanes[:, n * topk + k : n * topk + k + 1] for n in (1, 2))
                score = jnp.where(lanes[:, k : k + 1] == member, high + low, score)
            back = jnp.dot(
                chosen_ref[group], act_ref[group * slots : (group + 1) * slots, :], preferred_element_type=jnp.float32
            )
            gated_ref[group * rows : (group + 1) * rows, :] = (back * score).astype(jnp.bfloat16)

    @pl.when(step >= up_steps)
    def _():
        main_ref[...] = jnp.dot(
            act_ref[...], wout_ref[...], preferred_element_type=jnp.float32
        ).astype(main_ref.dtype)


def run_experts(member, rows, weight_in, weight_out, req_dev, cap, topk, main):
    width = weight_in.shape[1]
    hidden_dev = weight_out.shape[0]
    count = rows.shape[0]
    slots = count // req_dev * cap
    group = 16 * req_dev
    groups = count // group
    up, down = width // 7, 1536
    up_steps, down_steps = width // up, main // down

    def at_up(s):
        return (0, jnp.minimum(s, up_steps - 1))

    def at_down(s):
        return (0, jnp.maximum(s - up_steps, 0))

    return pl.pallas_call(
        functools.partial(expert_kernel, hidden_dev, req_dev, cap, topk, up_steps),
        out_shape=(
            jax.ShapeDtypeStruct((slots, main), jnp.bfloat16),
            jax.ShapeDtypeStruct((count, hidden_dev), jnp.bfloat16),
        ),
        grid=(up_steps + down_steps,),
        in_specs=[
            pl.BlockSpec(memory_space=pltpu.SMEM),
            pl.BlockSpec((count, ID_LANES), lambda s: (0, width // ID_LANES), pipeline_mode=pl.Buffered(1)),
            pl.BlockSpec((count, up), at_up),
            pl.BlockSpec((2 * hidden_dev, up), at_up),
            pl.BlockSpec((hidden_dev, down), at_down),
        ],
        out_specs=(
            pl.BlockSpec((slots, down), at_down),
            pl.BlockSpec((count, hidden_dev), lambda s: (0, 0)),
        ),
        scratch_shapes=[
            pltpu.VMEM((slots, 2 * hidden_dev), jnp.float32),
            pltpu.VMEM((groups, group, slots // groups), jnp.bfloat16),
            pltpu.VMEM((groups, slots // groups, group), jnp.bfloat16),
            pltpu.VMEM((slots, up), jnp.bfloat16),
            pltpu.VMEM((slots, hidden_dev), jnp.bfloat16),
        ],
        compiler_params=pltpu.CompilerParams(vmem_limit_bytes=52 * MIB),
        cost_estimate=pl.CostEstimate(
            flops=2 * slots * width * (2 * hidden_dev + group) + 2 * slots * hidden_dev * main,
            bytes_accessed=2 * (rows.size + weight_in.size + hidden_dev * main + slots * main + count * hidden_dev),
            transcendentals=slots * hidden_dev,
        ),
    )(member, rows, rows, weight_in, weight_out)


def reduce_side(gated, weight_out, req_dev):
    instances, chips = gated.shape[:2]
    cols = weight_out.shape[1]
    member = lax.axis_index("ffn")
    chip, core = member // 2, member % 2
    way = 1 - 2 * core
    ring = [(2 * z + c, 2 * ((z + 1 - 2 * c) % chips) + c) for z in range(chips) for c in range(2)]

    def part(target):
        rows = lax.dynamic_index_in_dim(gated, target, 1, keepdims=False).reshape(instances * req_dev, -1)
        return jnp.dot(rows, weight_out, preferred_element_type=jnp.float32)

    total = part((chip - way) % chips)
    for step in range(1, chips):
        arrived = lax.ppermute(total.astype(jnp.bfloat16), "ffn", ring)
        total = arrived.astype(jnp.float32) + part((chip - way * (1 + step)) % chips)
    spread = lax.all_to_all(
        total.astype(jnp.bfloat16).reshape(instances, req_dev, cols), "attn", split_axis=0, concat_axis=0, tiled=True
    )
    return jnp.sum(spread.astype(jnp.float32), axis=0)


def body(
    hidden,
    norm_gain,
    expert_ids,
    gate_scores,
    expert_in,
    expert_out,
    kv_pages,
    block_table,
    req_len,
    new_owner,
):
    req_dev = hidden.shape[0]
    width = hidden.shape[1]
    topk = expert_ids.shape[1]
    members = lax.axis_size("ffn")
    instances = lax.axis_size("attn")
    expert_cap = req_dev * topk * 4 // (members * 3)
    per_peer = 2 * req_dev // instances

    floats = hidden.astype(jnp.float32)
    scale = lax.rsqrt(jnp.mean(floats * floats, axis=-1, keepdims=True) + 1e-06)
    normed = (floats * scale * norm_gain).astype(jnp.bfloat16)
    gate_high = gate_scores.astype(jnp.bfloat16)
    gate_low = (gate_scores - gate_high.astype(jnp.float32)).astype(jnp.bfloat16)
    lanes = jnp.concatenate([expert_ids.astype(jnp.bfloat16), gate_high, gate_low], axis=1)
    lanes = jnp.pad(lanes, ((0, 0), (0, ID_LANES - 3 * topk)))
    payload = jnp.concatenate([normed, lanes], axis=1)
    payload, kv_pages = lax.optimization_barrier((payload, kv_pages))
    gathered = lax.all_gather(payload, ("attn", "ffn"), axis=0, tiled=True)

    owners = new_owner.reshape(-1)
    owner_hot = (owners[:, None] == jnp.arange(instances, dtype=jnp.int32)[None, :]).astype(
        jnp.int32
    )
    owner_rank = jnp.sum((jnp.cumsum(owner_hot, axis=0) - owner_hot) * owner_hot, axis=1)
    send_slot = owners * per_peer + owner_rank
    routing = jnp.arange(instances * per_peer, dtype=jnp.int32)[:, None] == send_slot[None, :]
    occupied = jnp.any(routing, axis=1)
    sources = jnp.sum(
        routing.astype(jnp.int32) * jnp.arange(req_dev, dtype=jnp.int32)[None, :], axis=1
    )
    tables = block_table[sources]
    page_rows = kv_pages[tables]
    positions = (
        jnp.arange(PAGES_REQ, dtype=jnp.int32)[:, None] * PAGE
        + jnp.arange(PAGE, dtype=jnp.int32)[None, :]
    )
    kept_mask = (positions[None, :, :] < req_len[sources][:, None, None]) & occupied[:, None, None]
    outgoing_pages = jnp.where(kept_mask[..., None], page_rows, jnp.zeros_like(page_rows))
    first_pages = lax.all_to_all(outgoing_pages[:, 0], "attn", split_axis=0, concat_axis=0, tiled=True)
    main = width - 2560
    swap = [(m, m ^ 1) for m in range(members)]
    weight_out = expert_out.reshape(expert_out.shape[1], width)
    side_out = weight_out[:, main:]
    side_out = jnp.concatenate([side_out, lax.ppermute(side_out, "ffn", swap)], axis=0)
    gathered, first_pages, second_out, side_out = lax.optimization_barrier(
        (gathered, first_pages, outgoing_pages[:, 1], side_out)
    )
    second_pages = lax.all_to_all(second_out, "attn", split_axis=0, concat_axis=0, tiled=True)
    member = lax.axis_index("ffn").astype(jnp.int32).reshape(1)
    hidden_dev = expert_in.shape[2]
    partial, gated = run_experts(
        member, gathered, expert_in.reshape(2 * hidden_dev, width), weight_out, req_dev, expert_cap, topk, main
    )
    partial, gated, second_pages = lax.optimization_barrier((partial, gated, second_pages))
    moved_pages = jnp.stack([first_pages, second_pages], axis=1)
    summed = lax.psum_scatter(partial, "attn", scatter_dimension=0, tiled=True)
    results = summed.reshape(members, expert_cap, main)
    returned = lax.all_to_all(results, "ffn", split_axis=0, concat_axis=0, tiled=True)

    gated = gated.reshape(instances, members // 2, 2, req_dev, hidden_dev)
    core = lax.axis_index("ffn") % 2
    own = lax.dynamic_index_in_dim(gated, core, 2, keepdims=False)
    other = lax.ppermute(lax.dynamic_index_in_dim(gated, 1 - core, 2, keepdims=False), "ffn", swap)
    side_mix = reduce_side(jnp.concatenate([own, other], axis=-1), side_out, req_dev)

    pair_ids = expert_ids.reshape(-1)
    onehot = (pair_ids[:, None] == jnp.arange(members, dtype=jnp.int32)[None, :]).astype(jnp.int32)
    rank_pos = jnp.sum((jnp.cumsum(onehot, axis=0) - onehot) * onehot, axis=1)
    slot_ids = pair_ids * expert_cap + rank_pos
    matches = jnp.arange(members * expert_cap, dtype=jnp.int32)[:, None] == slot_ids[None, :]
    matches = matches.reshape(members * expert_cap, req_dev, topk)
    combine_weights = jnp.einsum(
        "sjk,jk->js", matches.astype(jnp.float32), gate_scores, precision=lax.Precision.HIGHEST
    )
    main_mix = jnp.dot(
        combine_weights,
        returned.reshape(members * expert_cap, main).astype(jnp.float32),
        precision=lax.Precision.HIGHEST,
    )
    expert_mix = jnp.concatenate([main_mix, side_mix], axis=1)
    updated = (floats + expert_mix).astype(jnp.bfloat16)
    rows_out = jnp.dot(
        routing.astype(jnp.bfloat16), updated, preferred_element_type=jnp.float32
    ).astype(jnp.bfloat16)
    moved_rows = lax.all_to_all(rows_out, "attn", split_axis=0, concat_axis=0, tiled=True)
    return (moved_pages, moved_rows)


def solution(mesh):
    in_specs = (
        P(("attn", "ffn"), None),
        P(),
        P(("attn", "ffn"), None),
        P(("attn", "ffn"), None),
        P("ffn", None, "attn", None),
        P("ffn", "attn", None),
        P(("attn", "ffn"), None, None),
        P(("attn", "ffn"), None),
        P(("attn", "ffn")),
        P(("attn", "ffn"), None),
    )
    out_specs = (P(("attn", "ffn"), None, None, None), P(("attn", "ffn"), None))
    return jax.shard_map(body, mesh=mesh, in_specs=in_specs, out_specs=out_specs, check_vma=False)
```

```python
import functools

import jax
import jax.numpy as jnp
from jax import lax
from jax.experimental import pallas as pl
from jax.experimental.pallas import tpu as pltpu
from jax.sharding import PartitionSpec as P

PAGE = 64
PAGES_REQ = 2
ID_LANES = 128
MIB = 1 << 20


def payload_kernel(width, hidden_ref, gain_ref, ids_ref, gates_ref, out_ref, table_ref):
    floats = hidden_ref[...].astype(jnp.float32)
    scale = lax.rsqrt(jnp.mean(floats * floats, axis=-1, keepdims=True) + 1e-06)
    out_ref[:, :width] = (floats * scale * gain_ref[...]).astype(out_ref.dtype)
    topk, rows = ids_ref.shape
    gates = gates_ref[...]
    high = gates.astype(jnp.bfloat16).astype(jnp.float32)
    table_ref[...] = jnp.zeros_like(table_ref)
    for n, part in enumerate((ids_ref[...].astype(jnp.float32), high, gates - high)):
        table_ref[n * topk : (n + 1) * topk, :rows] = part
    out_ref[:, width:] = jnp.transpose(table_ref[...])[:rows, :].astype(out_ref.dtype)


def make_payload(hidden, gain, ids, gates):
    rows, width = hidden.shape
    return pl.pallas_call(
        functools.partial(payload_kernel, width),
        out_shape=jax.ShapeDtypeStruct((rows, width + ID_LANES), jnp.bfloat16),
        scratch_shapes=[pltpu.VMEM((ID_LANES, ID_LANES), jnp.float32)],
        compiler_params=pltpu.CompilerParams(vmem_limit_bytes=60 * MIB),
    )(hidden, gain.reshape(1, width), ids.T, gates.T)


def expert_kernel(
    hidden_dev, req_dev, cap, topk, up_steps,
    member_ref, lanes_ref, rows_ref, win_ref, wout_ref,
    main_ref, gated_ref,
    acc_ref, chosen_ref, pick_ref, picked_ref, act_ref,
):
    step = pl.program_id(0)
    groups, slots, rows = pick_ref.shape
    member = member_ref[0].astype(jnp.float32)

    @pl.when(step == 0)
    def _():
        first = lax.broadcasted_iota(jnp.int32, (rows, rows), 0)
        second = lax.broadcasted_iota(jnp.int32, (rows, rows), 1)
        before = jnp.where((second < first) & (second // req_dev == first // req_dev), 1.0, 0.0)
        block = lax.broadcasted_iota(jnp.int32, (rows, 1), 0) // req_dev
        slot = lax.broadcasted_iota(jnp.int32, (rows, slots), 1)
        for group in range(groups):
            lanes = lanes_ref[group * rows : (group + 1) * rows, :].astype(jnp.float32)
            lane = lax.broadcasted_iota(jnp.int32, lanes.shape, 1)
            hit = jnp.max(jnp.where((lanes == member) & (lane < topk), 1.0, 0.0), axis=1, keepdims=True)
            rank = jnp.dot(
                before.astype(jnp.bfloat16),
                jnp.broadcast_to(hit, (rows, 128)).astype(jnp.bfloat16),
                preferred_element_type=jnp.float32,
            )[:, :1]
            place = jnp.where(hit > 0.0, block * cap + rank.astype(jnp.int32), -1)
            chosen = jnp.where(place == slot, 1.0, 0.0)
            chosen_ref[group] = chosen.astype(jnp.bfloat16)
            pick_ref[group] = jnp.transpose(chosen).astype(jnp.bfloat16)
        acc_ref[...] = jnp.zeros_like(acc_ref)

    @pl.when(step < up_steps)
    def _():
        for group in range(groups):
            picked_ref[group * slots : (group + 1) * slots, :] = jnp.dot(
                pick_ref[group],
                rows_ref[group * rows : (group + 1) * rows, :],
                preferred_element_type=jnp.float32,
            ).astype(jnp.bfloat16)
        acc_ref[...] += lax.dot_general(
            picked_ref[...], win_ref[...], (((1,), (1,)), ((), ())), preferred_element_type=jnp.float32
        )

    @pl.when(step == up_steps - 1)
    def _():
        gate = acc_ref[:, :hidden_dev]
        act_ref[...] = (gate / (1.0 + jnp.exp(-gate)) * acc_ref[:, hidden_dev : 2 * hidden_dev]).astype(jnp.bfloat16)
        for group in range(groups):
            lanes = lanes_ref[group * rows : (group + 1) * rows, :].astype(jnp.float32)
            score = jnp.zeros((rows, 1), jnp.float32)
            for k in range(topk):
                high, low = (lanes[:, n * topk + k : n * topk + k + 1] for n in (1, 2))
                score = jnp.where(lanes[:, k : k + 1] == member, high + low, score)
            back = jnp.dot(
                chosen_ref[group], act_ref[group * slots : (group + 1) * slots, :], preferred_element_type=jnp.float32
            )
            gated_ref[group * rows : (group + 1) * rows, :] = (back * score).astype(jnp.bfloat16)

    @pl.when(step >= up_steps)
    def _():
        main_ref[...] = jnp.dot(
            act_ref[...], wout_ref[...], preferred_element_type=jnp.float32
        ).astype(main_ref.dtype)


def run_experts(member, rows, weight_in, weight_out, req_dev, cap, topk, main):
    width = weight_in.shape[1]
    hidden_dev = weight_out.shape[0]
    count = rows.shape[0]
    slots = count // req_dev * cap
    group = 16 * req_dev
    groups = count // group
    up, down = width // 7, 1536
    up_steps, down_steps = width // up, main // down

    def at_up(s):
        return (0, jnp.minimum(s, up_steps - 1))

    def at_down(s):
        return (0, jnp.maximum(s - up_steps, 0))

    return pl.pallas_call(
        functools.partial(expert_kernel, hidden_dev, req_dev, cap, topk, up_steps),
        out_shape=(
            jax.ShapeDtypeStruct((slots, main), jnp.bfloat16),
            jax.ShapeDtypeStruct((count, hidden_dev), jnp.bfloat16),
        ),
        grid=(up_steps + down_steps,),
        in_specs=[
            pl.BlockSpec(memory_space=pltpu.SMEM),
            pl.BlockSpec((count, ID_LANES), lambda s: (0, width // ID_LANES), pipeline_mode=pl.Buffered(1)),
            pl.BlockSpec((count, up), at_up),
            pl.BlockSpec((2 * hidden_dev, up), at_up),
            pl.BlockSpec((hidden_dev, down), at_down),
        ],
        out_specs=(
            pl.BlockSpec((slots, down), at_down),
            pl.BlockSpec((count, hidden_dev), lambda s: (0, 0)),
        ),
        scratch_shapes=[
            pltpu.VMEM((slots, 2 * hidden_dev), jnp.float32),
            pltpu.VMEM((groups, group, slots // groups), jnp.bfloat16),
            pltpu.VMEM((groups, slots // groups, group), jnp.bfloat16),
            pltpu.VMEM((slots, up), jnp.bfloat16),
            pltpu.VMEM((slots, hidden_dev), jnp.bfloat16),
        ],
        compiler_params=pltpu.CompilerParams(vmem_limit_bytes=52 * MIB),
        cost_estimate=pl.CostEstimate(
            flops=2 * slots * width * (2 * hidden_dev + group) + 2 * slots * hidden_dev * main,
            bytes_accessed=2 * (rows.size + weight_in.size + hidden_dev * main + slots * main + count * hidden_dev),
            transcendentals=slots * hidden_dev,
        ),
    )(member, rows, rows, weight_in, weight_out)


def reduce_side(gated, weight_out, req_dev):
    instances, chips = gated.shape[:2]
    cols = weight_out.shape[1]
    member = lax.axis_index("ffn")
    chip, core = member // 2, member % 2
    way = 1 - 2 * core
    ring = [(2 * z + c, 2 * ((z + 1 - 2 * c) % chips) + c) for z in range(chips) for c in range(2)]

    def part(target, span):
        rows = lax.dynamic_index_in_dim(gated, target, 1, keepdims=False).reshape(instances * req_dev, -1)
        return jnp.dot(rows, weight_out[:, span], preferred_element_type=jnp.float32)

    def ring_sum(span):
        total = part((chip - way) % chips, span)
        for step in range(1, chips):
            arrived = lax.ppermute(total.astype(jnp.bfloat16), "ffn", ring)
            total = arrived.astype(jnp.float32) + part((chip - way * (1 + step)) % chips, span)
        return total.astype(jnp.bfloat16)

    total = jnp.concatenate([ring_sum(slice(0, cols // 2)), ring_sum(slice(cols // 2, cols))], axis=1)
    spread = lax.all_to_all(
        total.reshape(instances, req_dev, cols), "attn", split_axis=0, concat_axis=0, tiled=True
    )
    return jnp.sum(spread.astype(jnp.float32), axis=0)


def body(
    hidden,
    norm_gain,
    expert_ids,
    gate_scores,
    expert_in,
    expert_out,
    kv_pages,
    block_table,
    req_len,
    new_owner,
):
    req_dev = hidden.shape[0]
    width = hidden.shape[1]
    topk = expert_ids.shape[1]
    members = lax.axis_size("ffn")
    instances = lax.axis_size("attn")
    expert_cap = req_dev * topk * 4 // (members * 3)
    per_peer = 2 * req_dev // instances

    floats = hidden.astype(jnp.float32)
    payload = make_payload(hidden, norm_gain, expert_ids, gate_scores)
    payload, kv_pages = lax.optimization_barrier((payload, kv_pages))
    gathered = lax.all_gather(payload, ("attn", "ffn"), axis=0, tiled=True)

    owners = new_owner.reshape(-1)
    owner_hot = (owners[:, None] == jnp.arange(instances, dtype=jnp.int32)[None, :]).astype(
        jnp.int32
    )
    owner_rank = jnp.sum((jnp.cumsum(owner_hot, axis=0) - owner_hot) * owner_hot, axis=1)
    send_slot = owners * per_peer + owner_rank
    routing = jnp.arange(instances * per_peer, dtype=jnp.int32)[:, None] == send_slot[None, :]
    occupied = jnp.any(routing, axis=1)
    sources = jnp.sum(
        routing.astype(jnp.int32) * jnp.arange(req_dev, dtype=jnp.int32)[None, :], axis=1
    )
    tables = block_table[sources]
    page_rows = kv_pages[tables]
    positions = (
        jnp.arange(PAGES_REQ, dtype=jnp.int32)[:, None] * PAGE
        + jnp.arange(PAGE, dtype=jnp.int32)[None, :]
    )
    kept_mask = (positions[None, :, :] < req_len[sources][:, None, None]) & occupied[:, None, None]
    outgoing_pages = jnp.where(kept_mask[..., None], page_rows, jnp.zeros_like(page_rows))
    first_pages = lax.all_to_all(outgoing_pages[:, 0], "attn", split_axis=0, concat_axis=0, tiled=True)
    main = width - 2560
    swap = [(m, m ^ 1) for m in range(members)]
    weight_out = expert_out.reshape(expert_out.shape[1], width)
    side_out = weight_out[:, main:]
    side_out = jnp.concatenate([side_out, lax.ppermute(side_out, "ffn", swap)], axis=0)
    gathered, first_pages, second_out, side_out = lax.optimization_barrier(
        (gathered, first_pages, outgoing_pages[:, 1], side_out)
    )
    second_pages = lax.all_to_all(second_out, "attn", split_axis=0, concat_axis=0, tiled=True)
    member = lax.axis_index("ffn").astype(jnp.int32).reshape(1)
    hidden_dev = expert_in.shape[2]
    partial, gated = run_experts(
        member, gathered, expert_in.reshape(2 * hidden_dev, width), weight_out, req_dev, expert_cap, topk, main
    )
    partial, gated, second_pages = lax.optimization_barrier((partial, gated, second_pages))
    moved_pages = jnp.stack([first_pages, second_pages], axis=1)
    summed = lax.psum_scatter(partial, "attn", scatter_dimension=0, tiled=True)
    results = summed.reshape(members, expert_cap, main)
    returned = lax.all_to_all(results, "ffn", split_axis=0, concat_axis=0, tiled=True)

    gated = gated.reshape(instances, members // 2, 2, req_dev, hidden_dev)
    core = lax.axis_index("ffn") % 2
    own = lax.dynamic_index_in_dim(gated, core, 2, keepdims=False)
    other = lax.ppermute(lax.dynamic_index_in_dim(gated, 1 - core, 2, keepdims=False), "ffn", swap)
    side_mix = reduce_side(jnp.concatenate([own, other], axis=-1), side_out, req_dev)

    pair_ids = expert_ids.reshape(-1)
    onehot = (pair_ids[:, None] == jnp.arange(members, dtype=jnp.int32)[None, :]).astype(jnp.int32)
    rank_pos = jnp.sum((jnp.cumsum(onehot, axis=0) - onehot) * onehot, axis=1)
    slot_ids = pair_ids * expert_cap + rank_pos
    matches = jnp.arange(members * expert_cap, dtype=jnp.int32)[:, None] == slot_ids[None, :]
    matches = matches.reshape(members * expert_cap, req_dev, topk)
    combine_weights = jnp.einsum(
        "sjk,jk->js", matches.astype(jnp.float32), gate_scores, precision=lax.Precision.HIGHEST
    )
    main_mix = jnp.dot(
        combine_weights,
        returned.reshape(members * expert_cap, main).astype(jnp.float32),
        precision=lax.Precision.HIGHEST,
    )
    expert_mix = jnp.concatenate([main_mix, side_mix], axis=1)
    updated = (floats + expert_mix).astype(jnp.bfloat16)
    rows_out = jnp.dot(
        routing.astype(jnp.bfloat16), updated, preferred_element_type=jnp.float32
    ).astype(jnp.bfloat16)
    moved_rows = lax.all_to_all(rows_out, "attn", split_axis=0, concat_axis=0, tiled=True)
    return (moved_pages, moved_rows)


def solution(mesh):
    in_specs = (
        P(("attn", "ffn"), None),
        P(),
        P(("attn", "ffn"), None),
        P(("attn", "ffn"), None),
        P("ffn", None, "attn", None),
        P("ffn", "attn", None),
        P(("attn", "ffn"), None, None),
        P(("attn", "ffn"), None),
        P(("attn", "ffn")),
        P(("attn", "ffn"), None),
    )
    out_specs = (P(("attn", "ffn"), None, None, None), P(("attn", "ffn"), None))
    return jax.shard_map(body, mesh=mesh, in_specs=in_specs, out_specs=out_specs, check_vma=False)
```

```python
import functools

import jax
import jax.numpy as jnp
from jax import lax
from jax.experimental import pallas as pl
from jax.experimental.pallas import tpu as pltpu
from jax.sharding import PartitionSpec as P

PAGE = 64
PAGES_REQ = 2
ID_LANES = 128
MIB = 1 << 20


def payload_kernel(width, hidden_ref, gain_ref, ids_ref, gates_ref, out_ref, table_ref):
    floats = hidden_ref[...].astype(jnp.float32)
    scale = lax.rsqrt(jnp.mean(floats * floats, axis=-1, keepdims=True) + 1e-06)
    out_ref[:, :width] = (floats * scale * gain_ref[...]).astype(out_ref.dtype)
    topk, rows = ids_ref.shape
    gates = gates_ref[...]
    high = gates.astype(jnp.bfloat16).astype(jnp.float32)
    table_ref[...] = jnp.zeros_like(table_ref)
    for n, part in enumerate((ids_ref[...].astype(jnp.float32), high, gates - high)):
        table_ref[n * topk : (n + 1) * topk, :rows] = part
    out_ref[:, width:] = jnp.transpose(table_ref[...])[:rows, :].astype(out_ref.dtype)


def make_payload(hidden, gain, ids, gates):
    rows, width = hidden.shape
    return pl.pallas_call(
        functools.partial(payload_kernel, width),
        out_shape=jax.ShapeDtypeStruct((rows, width + ID_LANES), jnp.bfloat16),
        scratch_shapes=[pltpu.VMEM((ID_LANES, ID_LANES), jnp.float32)],
        compiler_params=pltpu.CompilerParams(vmem_limit_bytes=60 * MIB),
    )(hidden, gain.reshape(1, width), ids.T, gates.T)


def expert_kernel(
    hidden_dev, req_dev, cap, topk, up_steps,
    member_ref, lanes_ref, rows_ref, win_ref, wout_ref,
    main_ref, gated_ref,
    acc_ref, chosen_ref, pick_ref, picked_ref, act_ref,
):
    step = pl.program_id(0)
    groups, slots, rows = pick_ref.shape
    member = member_ref[0].astype(jnp.float32)

    @pl.when(step == 0)
    def _():
        first = lax.broadcasted_iota(jnp.int32, (rows, rows), 0)
        second = lax.broadcasted_iota(jnp.int32, (rows, rows), 1)
        before = jnp.where((second < first) & (second // req_dev == first // req_dev), 1.0, 0.0)
        block = lax.broadcasted_iota(jnp.int32, (rows, 1), 0) // req_dev
        slot = lax.broadcasted_iota(jnp.int32, (rows, slots), 1)
        for group in range(groups):
            lanes = lanes_ref[group * rows : (group + 1) * rows, :].astype(jnp.float32)
            lane = lax.broadcasted_iota(jnp.int32, lanes.shape, 1)
            hit = jnp.max(jnp.where((lanes == member) & (lane < topk), 1.0, 0.0), axis=1, keepdims=True)
            rank = jnp.dot(
                before.astype(jnp.bfloat16),
                jnp.broadcast_to(hit, (rows, 128)).astype(jnp.bfloat16),
                preferred_element_type=jnp.float32,
            )[:, :1]
            place = jnp.where(hit > 0.0, block * cap + rank.astype(jnp.int32), -1)
            chosen = jnp.where(place == slot, 1.0, 0.0)
            chosen_ref[group] = chosen.astype(jnp.bfloat16)
            pick_ref[group] = jnp.transpose(chosen).astype(jnp.bfloat16)
        acc_ref[...] = jnp.zeros_like(acc_ref)

    @pl.when(step < up_steps)
    def _():
        for group in range(groups):
            picked_ref[group * slots : (group + 1) * slots, :] = jnp.dot(
                pick_ref[group],
                rows_ref[group * rows : (group + 1) * rows, :],
                preferred_element_type=jnp.float32,
            ).astype(jnp.bfloat16)
        acc_ref[...] += lax.dot_general(
            picked_ref[...], win_ref[...], (((1,), (1,)), ((), ())), preferred_element_type=jnp.float32
        )

    @pl.when(step == up_steps - 1)
    def _():
        gate = acc_ref[:, :hidden_dev]
        act_ref[...] = (gate / (1.0 + jnp.exp(-gate)) * acc_ref[:, hidden_dev : 2 * hidden_dev]).astype(jnp.bfloat16)
        for group in range(groups):
            lanes = lanes_ref[group * rows : (group + 1) * rows, :].astype(jnp.float32)
            score = jnp.zeros((rows, 1), jnp.float32)
            for k in range(topk):
                high, low = (lanes[:, n * topk + k : n * topk + k + 1] for n in (1, 2))
                score = jnp.where(lanes[:, k : k + 1] == member, high + low, score)
            back = jnp.dot(
                chosen_ref[group], act_ref[group * slots : (group + 1) * slots, :], preferred_element_type=jnp.float32
            )
            gated_ref[group * rows : (group + 1) * rows, :] = (back * score).astype(jnp.bfloat16)

    @pl.when(step >= up_steps)
    def _():
        main_ref[...] = jnp.dot(
            act_ref[...], wout_ref[...], preferred_element_type=jnp.float32
        ).astype(main_ref.dtype)


def run_experts(member, rows, weight_in, weight_out, req_dev, cap, topk, main):
    width = weight_in.shape[1]
    hidden_dev = weight_out.shape[0]
    count = rows.shape[0]
    slots = count // req_dev * cap
    group = 16 * req_dev
    groups = count // group
    up, down = width // 7, 1536
    up_steps, down_steps = width // up, main // down

    def at_up(s):
        return (0, jnp.minimum(s, up_steps - 1))

    def at_down(s):
        return (0, jnp.maximum(s - up_steps, 0))

    return pl.pallas_call(
        functools.partial(expert_kernel, hidden_dev, req_dev, cap, topk, up_steps),
        out_shape=(
            jax.ShapeDtypeStruct((slots, main), jnp.bfloat16),
            jax.ShapeDtypeStruct((count, hidden_dev), jnp.bfloat16),
        ),
        grid=(up_steps + down_steps,),
        in_specs=[
            pl.BlockSpec(memory_space=pltpu.SMEM),
            pl.BlockSpec((count, ID_LANES), lambda s: (0, width // ID_LANES), pipeline_mode=pl.Buffered(1)),
            pl.BlockSpec((count, up), at_up),
            pl.BlockSpec((2 * hidden_dev, up), at_up),
            pl.BlockSpec((hidden_dev, down), at_down),
        ],
        out_specs=(
            pl.BlockSpec((slots, down), at_down),
            pl.BlockSpec((count, hidden_dev), lambda s: (0, 0)),
        ),
        scratch_shapes=[
            pltpu.VMEM((slots, 2 * hidden_dev), jnp.float32),
            pltpu.VMEM((groups, group, slots // groups), jnp.bfloat16),
            pltpu.VMEM((groups, slots // groups, group), jnp.bfloat16),
            pltpu.VMEM((slots, up), jnp.bfloat16),
            pltpu.VMEM((slots, hidden_dev), jnp.bfloat16),
        ],
        compiler_params=pltpu.CompilerParams(vmem_limit_bytes=52 * MIB),
        cost_estimate=pl.CostEstimate(
            flops=2 * slots * width * (2 * hidden_dev + group) + 2 * slots * hidden_dev * main,
            bytes_accessed=2 * (rows.size + weight_in.size + hidden_dev * main + slots * main + count * hidden_dev),
            transcendentals=slots * hidden_dev,
        ),
    )(member, rows, rows, weight_in, weight_out)


def reduce_side(gated, weight_out, req_dev):
    instances, chips = gated.shape[:2]
    cols = weight_out.shape[1]
    member = lax.axis_index("ffn")
    chip, core = member // 2, member % 2
    way = 1 - 2 * core
    ring = [(2 * z + c, 2 * ((z + 1 - 2 * c) % chips) + c) for z in range(chips) for c in range(2)]

    def part(target, span):
        rows = lax.dynamic_index_in_dim(gated, target, 1, keepdims=False).reshape(instances * req_dev, -1)
        return jnp.dot(rows, weight_out[:, span], preferred_element_type=jnp.float32)

    def ring_sum(span):
        total = part((chip - way) % chips, span)
        for step in range(1, chips):
            arrived = lax.ppermute(total.astype(jnp.bfloat16), "ffn", ring)
            total = arrived.astype(jnp.float32) + part((chip - way * (1 + step)) % chips, span)
        return total.astype(jnp.bfloat16)

    total = jnp.concatenate([ring_sum(slice(0, cols // 2)), ring_sum(slice(cols // 2, cols))], axis=1)
    spread = lax.all_to_all(
        total.reshape(instances, req_dev, cols), "attn", split_axis=0, concat_axis=0, tiled=True
    )
    return jnp.sum(spread.astype(jnp.float32), axis=0)


def body(
    hidden,
    norm_gain,
    expert_ids,
    gate_scores,
    expert_in,
    expert_out,
    kv_pages,
    block_table,
    req_len,
    new_owner,
):
    req_dev = hidden.shape[0]
    width = hidden.shape[1]
    topk = expert_ids.shape[1]
    members = lax.axis_size("ffn")
    instances = lax.axis_size("attn")
    expert_cap = req_dev * topk * 4 // (members * 3)
    per_peer = 2 * req_dev // instances

    floats = hidden.astype(jnp.float32)
    payload = make_payload(hidden, norm_gain, expert_ids, gate_scores)
    payload, kv_pages = lax.optimization_barrier((payload, kv_pages))
    gathered = lax.all_gather(payload, ("attn", "ffn"), axis=0, tiled=True)

    owners = new_owner.reshape(-1)
    owner_hot = (owners[:, None] == jnp.arange(instances, dtype=jnp.int32)[None, :]).astype(
        jnp.int32
    )
    owner_rank = jnp.sum((jnp.cumsum(owner_hot, axis=0) - owner_hot) * owner_hot, axis=1)
    send_slot = owners * per_peer + owner_rank
    routing = jnp.arange(instances * per_peer, dtype=jnp.int32)[:, None] == send_slot[None, :]
    occupied = jnp.any(routing, axis=1)
    sources = jnp.sum(
        routing.astype(jnp.int32) * jnp.arange(req_dev, dtype=jnp.int32)[None, :], axis=1
    )
    tables = block_table[sources]
    page_rows = kv_pages[tables]
    positions = (
        jnp.arange(PAGES_REQ, dtype=jnp.int32)[:, None] * PAGE
        + jnp.arange(PAGE, dtype=jnp.int32)[None, :]
    )
    kept_mask = (positions[None, :, :] < req_len[sources][:, None, None]) & occupied[:, None, None]
    outgoing_pages = jnp.where(kept_mask[..., None], page_rows, jnp.zeros_like(page_rows))
    main = width - 2560
    swap = [(m, m ^ 1) for m in range(members)]
    weight_out = expert_out.reshape(expert_out.shape[1], width)
    side_out = weight_out[:, main:]
    side_out = jnp.concatenate([side_out, lax.ppermute(side_out, "ffn", swap)], axis=0)
    first_out, second_out, side_out = lax.optimization_barrier(
        (outgoing_pages[:, 0], outgoing_pages[:, 1], side_out)
    )
    first_pages = lax.all_to_all(first_out, "attn", split_axis=0, concat_axis=0, tiled=True)
    gathered, first_pages, second_out, side_out = lax.optimization_barrier(
        (gathered, first_pages, second_out, side_out)
    )
    second_pages = lax.all_to_all(second_out, "attn", split_axis=0, concat_axis=0, tiled=True)
    member = lax.axis_index("ffn").astype(jnp.int32).reshape(1)
    hidden_dev = expert_in.shape[2]
    partial, gated = run_experts(
        member, gathered, expert_in.reshape(2 * hidden_dev, width), weight_out, req_dev, expert_cap, topk, main
    )
    partial, gated, second_pages = lax.optimization_barrier((partial, gated, second_pages))
    moved_pages = jnp.stack([first_pages, second_pages], axis=1)
    summed = lax.psum_scatter(partial, "attn", scatter_dimension=0, tiled=True)
    results = summed.reshape(members, expert_cap, main)
    returned = lax.all_to_all(results, "ffn", split_axis=0, concat_axis=0, tiled=True)

    gated = gated.reshape(instances, members // 2, 2, req_dev, hidden_dev)
    core = lax.axis_index("ffn") % 2
    own = lax.dynamic_index_in_dim(gated, core, 2, keepdims=False)
    other = lax.ppermute(lax.dynamic_index_in_dim(gated, 1 - core, 2, keepdims=False), "ffn", swap)
    side_mix = reduce_side(jnp.concatenate([own, other], axis=-1), side_out, req_dev)

    pair_ids = expert_ids.reshape(-1)
    onehot = (pair_ids[:, None] == jnp.arange(members, dtype=jnp.int32)[None, :]).astype(jnp.int32)
    rank_pos = jnp.sum((jnp.cumsum(onehot, axis=0) - onehot) * onehot, axis=1)
    slot_ids = pair_ids * expert_cap + rank_pos
    matches = jnp.arange(members * expert_cap, dtype=jnp.int32)[:, None] == slot_ids[None, :]
    matches = matches.reshape(members * expert_cap, req_dev, topk)
    combine_weights = jnp.einsum(
        "sjk,jk->js", matches.astype(jnp.float32), gate_scores, precision=lax.Precision.HIGHEST
    )
    main_mix = jnp.dot(
        combine_weights,
        returned.reshape(members * expert_cap, main).astype(jnp.float32),
        precision=lax.Precision.HIGHEST,
    )
    expert_mix = jnp.concatenate([main_mix, side_mix], axis=1)
    updated = (floats + expert_mix).astype(jnp.bfloat16)
    rows_out = jnp.dot(
        routing.astype(jnp.bfloat16), updated, preferred_element_type=jnp.float32
    ).astype(jnp.bfloat16)
    moved_rows = lax.all_to_all(rows_out, "attn", split_axis=0, concat_axis=0, tiled=True)
    return (moved_pages, moved_rows)


def solution(mesh):
    in_specs = (
        P(("attn", "ffn"), None),
        P(),
        P(("attn", "ffn"), None),
        P(("attn", "ffn"), None),
        P("ffn", None, "attn", None),
        P("ffn", "attn", None),
        P(("attn", "ffn"), None, None),
        P(("attn", "ffn"), None),
        P(("attn", "ffn")),
        P(("attn", "ffn"), None),
    )
    out_specs = (P(("attn", "ffn"), None, None, None), P(("attn", "ffn"), None))
    return jax.shard_map(body, mesh=mesh, in_specs=in_specs, out_specs=out_specs, check_vma=False)
```

```python
import functools

import jax
import jax.numpy as jnp
from jax import lax
from jax.experimental import pallas as pl
from jax.experimental.pallas import tpu as pltpu
from jax.sharding import PartitionSpec as P

PAGE = 64
ID_LANES = 128
MIB = 1 << 20


def payload_kernel(width, hidden_ref, gain_ref, ids_ref, gates_ref, out_ref, table_ref):
    floats = hidden_ref[...].astype(jnp.float32)
    scale = lax.rsqrt(jnp.mean(floats * floats, axis=-1, keepdims=True) + 1e-06)
    out_ref[:, :width] = (floats * scale * gain_ref[...]).astype(out_ref.dtype)
    topk, rows = ids_ref.shape
    gates = gates_ref[...]
    high = gates.astype(jnp.bfloat16).astype(jnp.float32)
    table_ref[...] = jnp.zeros_like(table_ref)
    for n, part in enumerate((ids_ref[...].astype(jnp.float32), high, gates - high)):
        table_ref[n * topk : (n + 1) * topk, :rows] = part
    out_ref[:, width:] = jnp.transpose(table_ref[...])[:rows, :].astype(out_ref.dtype)


def make_payload(hidden, gain, ids, gates):
    rows, width = hidden.shape
    return pl.pallas_call(
        functools.partial(payload_kernel, width),
        out_shape=jax.ShapeDtypeStruct((rows, width + ID_LANES), jnp.bfloat16),
        scratch_shapes=[pltpu.VMEM((ID_LANES, ID_LANES), jnp.float32)],
        compiler_params=pltpu.CompilerParams(vmem_limit_bytes=60 * MIB),
    )(hidden, gain.reshape(1, width), ids.T, gates.T)


def expert_kernel(
    hidden_dev, req_dev, cap, topk, up_steps,
    member_ref, lanes_ref, rows_ref, win_ref, wout_ref,
    main_ref, gated_ref,
    acc_ref, chosen_ref, pick_ref, picked_ref, act_ref,
):
    step = pl.program_id(0)
    groups, slots, rows = pick_ref.shape
    member = member_ref[0].astype(jnp.float32)

    @pl.when(step == 0)
    def _():
        first = lax.broadcasted_iota(jnp.int32, (rows, rows), 0)
        second = lax.broadcasted_iota(jnp.int32, (rows, rows), 1)
        before = jnp.where((second < first) & (second // req_dev == first // req_dev), 1.0, 0.0)
        block = lax.broadcasted_iota(jnp.int32, (rows, 1), 0) // req_dev
        slot = lax.broadcasted_iota(jnp.int32, (rows, slots), 1)
        for group in range(groups):
            lanes = lanes_ref[group * rows : (group + 1) * rows, :].astype(jnp.float32)
            lane = lax.broadcasted_iota(jnp.int32, lanes.shape, 1)
            hit = jnp.max(jnp.where((lanes == member) & (lane < topk), 1.0, 0.0), axis=1, keepdims=True)
            rank = jnp.dot(
                before.astype(jnp.bfloat16),
                jnp.broadcast_to(hit, (rows, 128)).astype(jnp.bfloat16),
                preferred_element_type=jnp.float32,
            )[:, :1]
            place = jnp.where(hit > 0.0, block * cap + rank.astype(jnp.int32), -1)
            chosen = jnp.where(place == slot, 1.0, 0.0)
            chosen_ref[group] = chosen.astype(jnp.bfloat16)
            pick_ref[group] = jnp.transpose(chosen).astype(jnp.bfloat16)
        acc_ref[...] = jnp.zeros_like(acc_ref)

    @pl.when(step < up_steps)
    def _():
        for group in range(groups):
            picked_ref[group * slots : (group + 1) * slots, :] = jnp.dot(
                pick_ref[group],
                rows_ref[group * rows : (group + 1) * rows, :],
                preferred_element_type=jnp.float32,
            ).astype(jnp.bfloat16)
        acc_ref[...] += lax.dot_general(
            picked_ref[...], win_ref[...], (((1,), (1,)), ((), ())), preferred_element_type=jnp.float32
        )

    @pl.when(step == up_steps - 1)
    def _():
        gate = acc_ref[:, :hidden_dev]
        act_ref[...] = (gate / (1.0 + jnp.exp(-gate)) * acc_ref[:, hidden_dev : 2 * hidden_dev]).astype(jnp.bfloat16)
        source = lax.broadcasted_iota(jnp.int32, (ID_LANES, ID_LANES), 0)
        target = lax.broadcasted_iota(jnp.int32, (ID_LANES, ID_LANES), 1)
        moved = (target == source + topk) | (target == source + 2 * topk)
        shift = jnp.where(moved & (source < topk), 1.0, 0.0).astype(jnp.bfloat16)
        ones = jnp.ones((ID_LANES, hidden_dev), jnp.bfloat16)
        lane = lax.broadcasted_iota(jnp.int32, (rows, ID_LANES), 1)
        for group in range(groups):
            lanes = lanes_ref[group * rows : (group + 1) * rows, :].astype(jnp.float32)
            named = jnp.where((lanes == member) & (lane < topk), 1.0, 0.0).astype(jnp.bfloat16)
            parts = (jnp.dot(named, shift, preferred_element_type=jnp.float32) * lanes).astype(jnp.bfloat16)
            score = jnp.dot(parts, ones, preferred_element_type=jnp.float32)
            back = jnp.dot(
                chosen_ref[group], act_ref[group * slots : (group + 1) * slots, :], preferred_element_type=jnp.float32
            )
            gated_ref[group * rows : (group + 1) * rows, :] = (back * score).astype(jnp.bfloat16)

    @pl.when(step >= up_steps)
    def _():
        main_ref[...] = jnp.dot(
            act_ref[...], wout_ref[...], preferred_element_type=jnp.float32
        ).astype(main_ref.dtype)


def run_experts(member, rows, weight_in, weight_out, req_dev, cap, topk, main):
    width = weight_in.shape[1]
    hidden_dev = weight_out.shape[0]
    count = rows.shape[0]
    slots = count // req_dev * cap
    group = 16 * req_dev
    groups = count // group
    up, down = width // 7, 1536
    up_steps, down_steps = width // up, main // down

    def at_up(s):
        return (0, jnp.minimum(s, up_steps - 1))

    def at_down(s):
        return (0, jnp.maximum(s - up_steps, 0))

    return pl.pallas_call(
        functools.partial(expert_kernel, hidden_dev, req_dev, cap, topk, up_steps),
        out_shape=(
            jax.ShapeDtypeStruct((slots, main), jnp.bfloat16),
            jax.ShapeDtypeStruct((count, hidden_dev), jnp.bfloat16),
        ),
        grid=(up_steps + down_steps,),
        in_specs=[
            pl.BlockSpec(memory_space=pltpu.SMEM),
            pl.BlockSpec((count, ID_LANES), lambda s: (0, width // ID_LANES), pipeline_mode=pl.Buffered(1)),
            pl.BlockSpec((count, up), at_up),
            pl.BlockSpec((2 * hidden_dev, up), at_up),
            pl.BlockSpec((hidden_dev, down), at_down),
        ],
        out_specs=(
            pl.BlockSpec((slots, down), at_down),
            pl.BlockSpec((count, hidden_dev), lambda s: (0, 0)),
        ),
        scratch_shapes=[
            pltpu.VMEM((slots, 2 * hidden_dev), jnp.float32),
            pltpu.VMEM((groups, group, slots // groups), jnp.bfloat16),
            pltpu.VMEM((groups, slots // groups, group), jnp.bfloat16),
            pltpu.VMEM((slots, up), jnp.bfloat16),
            pltpu.VMEM((slots, hidden_dev), jnp.bfloat16),
        ],
        compiler_params=pltpu.CompilerParams(vmem_limit_bytes=52 * MIB),
        cost_estimate=pl.CostEstimate(
            flops=2 * slots * width * (2 * hidden_dev + group) + 2 * slots * hidden_dev * main,
            bytes_accessed=2 * (rows.size + weight_in.size + hidden_dev * main + slots * main + count * hidden_dev),
            transcendentals=slots * hidden_dev,
        ),
    )(member, rows, rows, weight_in, weight_out)


def reduce_side(gated, weight_out, req_dev):
    instances, chips = gated.shape[:2]
    cols = weight_out.shape[1]
    member = lax.axis_index("ffn")
    chip, core = member // 2, member % 2
    way = 1 - 2 * core
    ring = [(2 * z + c, 2 * ((z + 1 - 2 * c) % chips) + c) for z in range(chips) for c in range(2)]

    def part(target, span):
        rows = lax.dynamic_index_in_dim(gated, target, 1, keepdims=False).reshape(instances * req_dev, -1)
        return jnp.dot(rows, weight_out[:, span], preferred_element_type=jnp.float32)

    def ring_sum(span):
        total = part((chip - way) % chips, span)
        for step in range(1, chips):
            arrived = lax.ppermute(total.astype(jnp.bfloat16), "ffn", ring)
            total = arrived.astype(jnp.float32) + part((chip - way * (1 + step)) % chips, span)
        return total.astype(jnp.bfloat16)

    total = jnp.concatenate([ring_sum(slice(0, cols // 2)), ring_sum(slice(cols // 2, cols))], axis=1)
    spread = lax.all_to_all(
        total.reshape(instances, req_dev, cols), "attn", split_axis=0, concat_axis=0, tiled=True
    )
    return jnp.sum(spread.astype(jnp.float32), axis=0)


def body(
    hidden,
    norm_gain,
    expert_ids,
    gate_scores,
    expert_in,
    expert_out,
    kv_pages,
    block_table,
    req_len,
    new_owner,
):
    req_dev = hidden.shape[0]
    width = hidden.shape[1]
    topk = expert_ids.shape[1]
    members = lax.axis_size("ffn")
    instances = lax.axis_size("attn")
    expert_cap = req_dev * topk * 4 // (members * 3)
    per_peer = 2 * req_dev // instances

    floats = hidden.astype(jnp.float32)
    payload = make_payload(hidden, norm_gain, expert_ids, gate_scores)
    payload, kv_pages = lax.optimization_barrier((payload, kv_pages))
    gathered = lax.all_gather(payload, ("attn", "ffn"), axis=0, tiled=True)

    owners = new_owner.reshape(-1)
    owner_hot = (owners[:, None] == jnp.arange(instances, dtype=jnp.int32)[None, :]).astype(
        jnp.int32
    )
    owner_rank = jnp.sum((jnp.cumsum(owner_hot, axis=0) - owner_hot) * owner_hot, axis=1)
    send_slot = owners * per_peer + owner_rank
    routing = jnp.arange(instances * per_peer, dtype=jnp.int32)[:, None] == send_slot[None, :]
    occupied = jnp.any(routing, axis=1)
    sources = jnp.sum(
        routing.astype(jnp.int32) * jnp.arange(req_dev, dtype=jnp.int32)[None, :], axis=1
    )
    tables = block_table[sources]
    def pages_out(pages, which):
        positions = which * PAGE + jnp.arange(PAGE, dtype=jnp.int32)
        kept_mask = (positions[None, :] < req_len[sources][:, None]) & occupied[:, None]
        page_rows = pages[tables[:, which]]
        return jnp.where(kept_mask[..., None], page_rows, jnp.zeros_like(page_rows))

    first_pages = lax.all_to_all(pages_out(kv_pages, 0), "attn", split_axis=0, concat_axis=0, tiled=True)
    first_pages, kv_pages, expert_out = lax.optimization_barrier((first_pages, kv_pages, expert_out))
    second_out = pages_out(kv_pages, 1)

    main = width - 2560
    swap = [(m, m ^ 1) for m in range(members)]
    weight_out = expert_out.reshape(expert_out.shape[1], width)
    side_out = weight_out[:, main:]
    side_out = jnp.concatenate([side_out, lax.ppermute(side_out, "ffn", swap)], axis=0)
    gathered, first_pages, second_out, side_out = lax.optimization_barrier(
        (gathered, first_pages, second_out, side_out)
    )
    second_pages = lax.all_to_all(second_out, "attn", split_axis=0, concat_axis=0, tiled=True)
    member = lax.axis_index("ffn").astype(jnp.int32).reshape(1)
    hidden_dev = expert_in.shape[2]
    partial, gated = run_experts(
        member, gathered, expert_in.reshape(2 * hidden_dev, width), weight_out, req_dev, expert_cap, topk, main
    )
    partial, gated, second_pages = lax.optimization_barrier((partial, gated, second_pages))
    moved_pages = jnp.stack([first_pages, second_pages], axis=1)
    summed = lax.psum_scatter(partial, "attn", scatter_dimension=0, tiled=True)
    results = summed.reshape(members, expert_cap, main)
    returned = lax.all_to_all(results, "ffn", split_axis=0, concat_axis=0, tiled=True)

    gated = gated.reshape(instances, members // 2, 2, req_dev, hidden_dev)
    core = lax.axis_index("ffn") % 2
    own = lax.dynamic_index_in_dim(gated, core, 2, keepdims=False)
    other = lax.ppermute(lax.dynamic_index_in_dim(gated, 1 - core, 2, keepdims=False), "ffn", swap)
    side_mix = reduce_side(jnp.concatenate([own, other], axis=-1), side_out, req_dev)

    pair_ids = expert_ids.reshape(-1)
    onehot = (pair_ids[:, None] == jnp.arange(members, dtype=jnp.int32)[None, :]).astype(jnp.int32)
    rank_pos = jnp.sum((jnp.cumsum(onehot, axis=0) - onehot) * onehot, axis=1)
    slot_ids = pair_ids * expert_cap + rank_pos
    matches = jnp.arange(members * expert_cap, dtype=jnp.int32)[:, None] == slot_ids[None, :]
    matches = matches.reshape(members * expert_cap, req_dev, topk)
    combine_weights = jnp.einsum(
        "sjk,jk->js", matches.astype(jnp.float32), gate_scores, precision=lax.Precision.HIGHEST
    )
    main_mix = jnp.dot(
        combine_weights,
        returned.reshape(members * expert_cap, main).astype(jnp.float32),
        precision=lax.Precision.HIGHEST,
    )
    expert_mix = jnp.concatenate([main_mix, side_mix], axis=1)
    updated = (floats + expert_mix).astype(jnp.bfloat16)
    rows_out = jnp.dot(
        routing.astype(jnp.bfloat16), updated, preferred_element_type=jnp.float32
    ).astype(jnp.bfloat16)
    moved_rows = lax.all_to_all(rows_out, "attn", split_axis=0, concat_axis=0, tiled=True)
    return (moved_pages, moved_rows)


def solution(mesh):
    in_specs = (
        P(("attn", "ffn"), None),
        P(),
        P(("attn", "ffn"), None),
        P(("attn", "ffn"), None),
        P("ffn", None, "attn", None),
        P("ffn", "attn", None),
        P(("attn", "ffn"), None, None),
        P(("attn", "ffn"), None),
        P(("attn", "ffn")),
        P(("attn", "ffn"), None),
    )
    out_specs = (P(("attn", "ffn"), None, None, None), P(("attn", "ffn"), None))
    return jax.shard_map(body, mesh=mesh, in_specs=in_specs, out_specs=out_specs, check_vma=False)
```

```python
import functools

import jax
import jax.numpy as jnp
from jax import lax
from jax.experimental import pallas as pl
from jax.experimental.pallas import tpu as pltpu
from jax.sharding import PartitionSpec as P

PAGE = 64
ID_LANES = 128
MIB = 1 << 20


def payload_kernel(width, hidden_ref, gain_ref, ids_ref, gates_ref, out_ref, table_ref):
    floats = hidden_ref[...].astype(jnp.float32)
    scale = lax.rsqrt(jnp.mean(floats * floats, axis=-1, keepdims=True) + 1e-06)
    out_ref[:, :width] = (floats * scale * gain_ref[...]).astype(out_ref.dtype)
    topk, rows = ids_ref.shape
    gates = gates_ref[...]
    high = gates.astype(jnp.bfloat16).astype(jnp.float32)
    table_ref[...] = jnp.zeros_like(table_ref)
    for n, part in enumerate((ids_ref[...].astype(jnp.float32), high, gates - high)):
        table_ref[n * topk : (n + 1) * topk, :rows] = part
    out_ref[:, width:] = jnp.transpose(table_ref[...])[:rows, :].astype(out_ref.dtype)


def make_payload(hidden, gain, ids, gates):
    rows, width = hidden.shape
    return pl.pallas_call(
        functools.partial(payload_kernel, width),
        out_shape=jax.ShapeDtypeStruct((rows, width + ID_LANES), jnp.bfloat16),
        scratch_shapes=[pltpu.VMEM((ID_LANES, ID_LANES), jnp.float32)],
        compiler_params=pltpu.CompilerParams(vmem_limit_bytes=60 * MIB),
    )(hidden, gain.reshape(1, width), ids.T, gates.T)


def expert_kernel(
    hidden_dev, req_dev, cap, topk, up_steps,
    member_ref, lanes_ref, rows_ref, win_ref, wout_ref,
    main_ref, gated_ref,
    acc_ref, chosen_ref, pick_ref, picked_ref, act_ref,
):
    step = pl.program_id(0)
    groups, slots, rows = pick_ref.shape
    member = member_ref[0].astype(jnp.float32)

    @pl.when(step == 0)
    def _():
        first = lax.broadcasted_iota(jnp.int32, (rows, rows), 0)
        second = lax.broadcasted_iota(jnp.int32, (rows, rows), 1)
        before = jnp.where((second < first) & (second // req_dev == first // req_dev), 1.0, 0.0)
        block = lax.broadcasted_iota(jnp.int32, (rows, 1), 0) // req_dev
        slot = lax.broadcasted_iota(jnp.int32, (rows, slots), 1)
        for group in range(groups):
            lanes = lanes_ref[group * rows : (group + 1) * rows, :].astype(jnp.float32)
            lane = lax.broadcasted_iota(jnp.int32, lanes.shape, 1)
            hit = jnp.max(jnp.where((lanes == member) & (lane < topk), 1.0, 0.0), axis=1, keepdims=True)
            rank = jnp.dot(
                before.astype(jnp.bfloat16),
                jnp.broadcast_to(hit, (rows, 128)).astype(jnp.bfloat16),
                preferred_element_type=jnp.float32,
            )[:, :1]
            place = jnp.where(hit > 0.0, block * cap + rank.astype(jnp.int32), -1)
            chosen = jnp.where(place == slot, 1.0, 0.0)
            chosen_ref[group] = chosen.astype(jnp.bfloat16)
            pick_ref[group] = jnp.transpose(chosen).astype(jnp.bfloat16)
        acc_ref[...] = jnp.zeros_like(acc_ref)

    @pl.when(step < up_steps)
    def _():
        for group in range(groups):
            picked_ref[group * slots : (group + 1) * slots, :] = jnp.dot(
                pick_ref[group],
                rows_ref[group * rows : (group + 1) * rows, :],
                preferred_element_type=jnp.float32,
            ).astype(jnp.bfloat16)
        acc_ref[...] += lax.dot_general(
            picked_ref[...], win_ref[...], (((1,), (1,)), ((), ())), preferred_element_type=jnp.float32
        )

    @pl.when(step == up_steps - 1)
    def _():
        gate = acc_ref[:, :hidden_dev]
        act_ref[...] = (gate / (1.0 + jnp.exp(-gate)) * acc_ref[:, hidden_dev : 2 * hidden_dev]).astype(jnp.bfloat16)
        source = lax.broadcasted_iota(jnp.int32, (ID_LANES, ID_LANES), 0)
        target = lax.broadcasted_iota(jnp.int32, (ID_LANES, ID_LANES), 1)
        moved = (target == source + topk) | (target == source + 2 * topk)
        shift = jnp.where(moved & (source < topk), 1.0, 0.0).astype(jnp.bfloat16)
        ones = jnp.ones((ID_LANES, hidden_dev), jnp.bfloat16)
        lane = lax.broadcasted_iota(jnp.int32, (rows, ID_LANES), 1)
        for group in range(groups):
            lanes = lanes_ref[group * rows : (group + 1) * rows, :].astype(jnp.float32)
            named = jnp.where((lanes == member) & (lane < topk), 1.0, 0.0).astype(jnp.bfloat16)
            parts = (jnp.dot(named, shift, preferred_element_type=jnp.float32) * lanes).astype(jnp.bfloat16)
            score = jnp.dot(parts, ones, preferred_element_type=jnp.float32)
            back = jnp.dot(
                chosen_ref[group], act_ref[group * slots : (group + 1) * slots, :], preferred_element_type=jnp.float32
            )
            gated_ref[group * rows : (group + 1) * rows, :] = (back * score).astype(jnp.bfloat16)

    @pl.when(step >= up_steps)
    def _():
        main_ref[...] = jnp.dot(
            act_ref[...], wout_ref[...], preferred_element_type=jnp.float32
        ).astype(main_ref.dtype)


def run_experts(member, rows, weight_in, weight_out, req_dev, cap, topk, main):
    width = weight_in.shape[1]
    hidden_dev = weight_out.shape[0]
    count = rows.shape[0]
    slots = count // req_dev * cap
    group = 16 * req_dev
    groups = count // group
    up, down = width // 7, 2304
    up_steps, down_steps = width // up, main // down

    def at_up(s):
        return (0, jnp.minimum(s, up_steps - 1))

    def at_down(s):
        return (0, jnp.maximum(s - up_steps, 0))

    return pl.pallas_call(
        functools.partial(expert_kernel, hidden_dev, req_dev, cap, topk, up_steps),
        out_shape=(
            jax.ShapeDtypeStruct((slots, main), jnp.bfloat16),
            jax.ShapeDtypeStruct((count, hidden_dev), jnp.bfloat16),
        ),
        grid=(up_steps + down_steps,),
        in_specs=[
            pl.BlockSpec(memory_space=pltpu.SMEM),
            pl.BlockSpec((count, ID_LANES), lambda s: (0, width // ID_LANES), pipeline_mode=pl.Buffered(1)),
            pl.BlockSpec((count, up), at_up),
            pl.BlockSpec((2 * hidden_dev, up), at_up),
            pl.BlockSpec((hidden_dev, down), at_down),
        ],
        out_specs=(
            pl.BlockSpec((slots, down), at_down),
            pl.BlockSpec((count, hidden_dev), lambda s: (0, 0)),
        ),
        scratch_shapes=[
            pltpu.VMEM((slots, 2 * hidden_dev), jnp.float32),
            pltpu.VMEM((groups, group, slots // groups), jnp.bfloat16),
            pltpu.VMEM((groups, slots // groups, group), jnp.bfloat16),
            pltpu.VMEM((slots, up), jnp.bfloat16),
            pltpu.VMEM((slots, hidden_dev), jnp.bfloat16),
        ],
        compiler_params=pltpu.CompilerParams(vmem_limit_bytes=52 * MIB),
        cost_estimate=pl.CostEstimate(
            flops=2 * slots * width * (2 * hidden_dev + group) + 2 * slots * hidden_dev * main,
            bytes_accessed=2 * (rows.size + weight_in.size + hidden_dev * main + slots * main + count * hidden_dev),
            transcendentals=slots * hidden_dev,
        ),
    )(member, rows, rows, weight_in, weight_out)


def reduce_side(gated, weight_out, req_dev):
    instances, chips = gated.shape[:2]
    cols = weight_out.shape[1]
    member = lax.axis_index("ffn")
    chip, core = member // 2, member % 2
    way = 1 - 2 * core
    ring = [(2 * z + c, 2 * ((z + 1 - 2 * c) % chips) + c) for z in range(chips) for c in range(2)]

    def part(target, span):
        rows = lax.dynamic_index_in_dim(gated, target, 1, keepdims=False).reshape(instances * req_dev, -1)
        return jnp.dot(rows, weight_out[:, span], preferred_element_type=jnp.float32)

    def ring_sum(span):
        total = part((chip - way) % chips, span)
        for step in range(1, chips):
            arrived = lax.ppermute(total.astype(jnp.bfloat16), "ffn", ring)
            total = arrived.astype(jnp.float32) + part((chip - way * (1 + step)) % chips, span)
        return total.astype(jnp.bfloat16)

    total = jnp.concatenate([ring_sum(slice(0, cols // 2)), ring_sum(slice(cols // 2, cols))], axis=1)
    spread = lax.all_to_all(
        total.reshape(instances, req_dev, cols), "attn", split_axis=0, concat_axis=0, tiled=True
    )
    return jnp.sum(spread.astype(jnp.float32), axis=0)


def body(
    hidden,
    norm_gain,
    expert_ids,
    gate_scores,
    expert_in,
    expert_out,
    kv_pages,
    block_table,
    req_len,
    new_owner,
):
    req_dev = hidden.shape[0]
    width = hidden.shape[1]
    topk = expert_ids.shape[1]
    members = lax.axis_size("ffn")
    instances = lax.axis_size("attn")
    expert_cap = req_dev * topk * 4 // (members * 3)
    per_peer = 2 * req_dev // instances

    floats = hidden.astype(jnp.float32)
    payload = make_payload(hidden, norm_gain, expert_ids, gate_scores)
    payload, kv_pages = lax.optimization_barrier((payload, kv_pages))
    gathered = lax.all_gather(payload, ("attn", "ffn"), axis=0, tiled=True)

    owners = new_owner.reshape(-1)
    owner_hot = (owners[:, None] == jnp.arange(instances, dtype=jnp.int32)[None, :]).astype(
        jnp.int32
    )
    owner_rank = jnp.sum((jnp.cumsum(owner_hot, axis=0) - owner_hot) * owner_hot, axis=1)
    send_slot = owners * per_peer + owner_rank
    routing = jnp.arange(instances * per_peer, dtype=jnp.int32)[:, None] == send_slot[None, :]
    occupied = jnp.any(routing, axis=1)
    sources = jnp.sum(
        routing.astype(jnp.int32) * jnp.arange(req_dev, dtype=jnp.int32)[None, :], axis=1
    )
    tables = block_table[sources]
    def pages_out(pages, which):
        positions = which * PAGE + jnp.arange(PAGE, dtype=jnp.int32)
        kept_mask = (positions[None, :] < req_len[sources][:, None]) & occupied[:, None]
        page_rows = pages[tables[:, which]]
        return jnp.where(kept_mask[..., None], page_rows, jnp.zeros_like(page_rows))

    first_pages = lax.all_to_all(pages_out(kv_pages, 0), "attn", split_axis=0, concat_axis=0, tiled=True)
    first_pages, kv_pages, expert_out = lax.optimization_barrier((first_pages, kv_pages, expert_out))
    second_out = pages_out(kv_pages, 1)

    main = width - 2560
    swap = [(m, m ^ 1) for m in range(members)]
    weight_out = expert_out.reshape(expert_out.shape[1], width)
    side_out = weight_out[:, main:]
    side_out = jnp.concatenate([side_out, lax.ppermute(side_out, "ffn", swap)], axis=0)
    gathered, first_pages, second_out, side_out = lax.optimization_barrier(
        (gathered, first_pages, second_out, side_out)
    )
    second_pages = lax.all_to_all(second_out, "attn", split_axis=0, concat_axis=0, tiled=True)
    member = lax.axis_index("ffn").astype(jnp.int32).reshape(1)
    hidden_dev = expert_in.shape[2]
    partial, gated = run_experts(
        member, gathered, expert_in.reshape(2 * hidden_dev, width), weight_out, req_dev, expert_cap, topk, main
    )
    partial, gated, second_pages = lax.optimization_barrier((partial, gated, second_pages))
    moved_pages = jnp.stack([first_pages, second_pages], axis=1)
    summed = lax.psum_scatter(partial, "attn", scatter_dimension=0, tiled=True)
    results = summed.reshape(members, expert_cap, main)
    returned = lax.all_to_all(results, "ffn", split_axis=0, concat_axis=0, tiled=True)

    gated = gated.reshape(instances, members // 2, 2, req_dev, hidden_dev)
    core = lax.axis_index("ffn") % 2
    own = lax.dynamic_index_in_dim(gated, core, 2, keepdims=False)
    other = lax.ppermute(lax.dynamic_index_in_dim(gated, 1 - core, 2, keepdims=False), "ffn", swap)
    side_mix = reduce_side(jnp.concatenate([own, other], axis=-1), side_out, req_dev)

    pair_ids = expert_ids.reshape(-1)
    onehot = (pair_ids[:, None] == jnp.arange(members, dtype=jnp.int32)[None, :]).astype(jnp.int32)
    rank_pos = jnp.sum((jnp.cumsum(onehot, axis=0) - onehot) * onehot, axis=1)
    slot_ids = pair_ids * expert_cap + rank_pos
    matches = jnp.arange(members * expert_cap, dtype=jnp.int32)[:, None] == slot_ids[None, :]
    matches = matches.reshape(members * expert_cap, req_dev, topk)
    combine_weights = jnp.einsum(
        "sjk,jk->js", matches.astype(jnp.float32), gate_scores, precision=lax.Precision.HIGHEST
    )
    main_mix = jnp.dot(
        combine_weights,
        returned.reshape(members * expert_cap, main).astype(jnp.float32),
        precision=lax.Precision.HIGHEST,
    )
    expert_mix = jnp.concatenate([main_mix, side_mix], axis=1)
    updated = (floats + expert_mix).astype(jnp.bfloat16)
    rows_out = jnp.dot(
        routing.astype(jnp.bfloat16), updated, preferred_element_type=jnp.float32
    ).astype(jnp.bfloat16)
    moved_rows = lax.all_to_all(rows_out, "attn", split_axis=0, concat_axis=0, tiled=True)
    return (moved_pages, moved_rows)


def solution(mesh):
    in_specs = (
        P(("attn", "ffn"), None),
        P(),
        P(("attn", "ffn"), None),
        P(("attn", "ffn"), None),
        P("ffn", None, "attn", None),
        P("ffn", "attn", None),
        P(("attn", "ffn"), None, None),
        P(("attn", "ffn"), None),
        P(("attn", "ffn")),
        P(("attn", "ffn"), None),
    )
    out_specs = (P(("attn", "ffn"), None, None, None), P(("attn", "ffn"), None))
    return jax.shard_map(body, mesh=mesh, in_specs=in_specs, out_specs=out_specs, check_vma=False)
```
